128 devices in a mesh: head: 4 (over x), wide: 32 (over y, z, core).
Axes of the slice: x: 4, y: 4, z: 4, core: 2. Of those that a mesh axis runs over, the one named last changes fastest.
Arguments:
- kv_cache: bfloat16 [64, 8192, 1024], P(None, 'wide', 'head'), may hold values from -8 to 8, as said below
- lin_states: float32 [64, 32, 128, 128], P(None, 'head', 'wide'), may hold values from -6 to 6
- row_order: int32 [64], replicated, may hold values from 0 to 63, each once
- prompt_lengths: int32 [64], replicated, may hold values from 512 to 8192, as said below
- att_query: bfloat16 [64, 3, 16, 256], P('wide'), may hold values from -8 to 8
- new_kv: bfloat16 [64, 3, 1024], P('wide'), may hold values from -6 to 6
- att_gate: bfloat16 [64, 3, 4096], P('wide', None, 'head'), may hold values from -6 to 6
- lin_query: bfloat16 [64, 3, 16, 128], P('wide', None, 'head'), may hold values from -6 to 6
- lin_key: bfloat16 [64, 3, 16, 128], P('wide', None, 'head'), may hold values from -6 to 6
- lin_value: bfloat16 [64, 3, 32, 128], P('wide', None, 'head'), may hold values from -6 to 6
- lin_decay: float32 [64, 3, 32], P('wide', None, 'head'), may hold values from 0.3 to 1
- lin_beta: float32 [64, 3, 32], P('wide', None, 'head'), may hold values from 0.2 to 1
- lin_gate: bfloat16 [64, 3, 32, 128], P('wide', None, 'head'), may hold values from -6 to 6
Outputs:
- att_out: bfloat16 [64, 3, 4096], P('wide', None, 'head')
- lin_out: bfloat16 [64, 3, 32, 128], P('wide', None, 'head')
- final_states: float32 [64, 32, 128, 128], P('wide', 'head')
The draws below stay inside these ranges and needn't reach their ends.
Inputs may be any that keep to these rules, and one draw needn't show every extreme that they name: `kv_cache`: keys and values of every prompt position, also beyond a row's length. `row_order`: each prefill row appears once. `prompt_lengths`: some row has length 8192.
All inputs are finite; a program needn't handle non-finite values.
Results may differ from the reference program's by a relative error of at most 0.015.
Values may be sent and summed in bfloat16 or wider, within the bound.
No kernel may reach another device: no remote copies, remote signals or barrier semaphores. Data moves between devices by JAX's collectives and lax.ppermute only.
A program may use at most 128 MiB of HBM per device.

```python
import jax
import jax.numpy as jnp
from jax import lax

HEADS_V = 32
HEADS_K = 16
DK = 128
DV = 128
HQ = 16
KVH = 2
HD = 256
STEPS = 3
LEN = 8192
ROWS = 64
FEAT = 1024


def draw_kv_cache(key, part):
    key = jax.random.fold_in(key, 1)
    base = jnp.clip(jax.random.normal(key, (ROWS, LEN, FEAT), jnp.float32), -6.0, 6.0)
    return base.astype(jnp.bfloat16)


def draw_att_query(key, part):
    key = jax.random.fold_in(key, 2)
    base = jnp.clip(jax.random.normal(key, (ROWS, STEPS, HQ, HD), jnp.float32), -6.0, 6.0)
    return base.astype(jnp.bfloat16)


def draw_prompt_lengths(key, part):
    key = jax.random.fold_in(key, 3)
    first, second, third = jax.random.split(key, 3)
    powers = jax.random.randint(first, (ROWS,), 0, 4)
    minus = jax.random.randint(second, (ROWS,), 0, LEN // 16)
    lengths = jnp.right_shift(jnp.full((ROWS,), LEN, jnp.int32), powers.astype(jnp.int32)) - minus
    longest = jax.random.randint(third, (), 0, ROWS)
    return jnp.where(jnp.arange(ROWS) == longest, LEN, lengths).astype(jnp.int32)


def block_levels(rng, dims, cuts, least, largest):
    def one(axis_at, shards_of):
        heights = jax.random.uniform(jax.random.fold_in(jax.random.fold_in(rng, 6), axis_at), (shards_of,), jnp.float32, least / len(cuts), largest / len(cuts))
        return jnp.repeat(jnp.exp(heights), dims[axis_at] // shards_of).reshape((-1,) + (1,) * (len(dims) - axis_at - 1))

    factor_of = one(*cuts[0])
    for cut in cuts[1:]:
        factor_of = factor_of * one(*cut)
    return factor_of


def scatter_about(rng, dims, deviation, limit, cuts=(), kind=jnp.bfloat16):
    level = block_levels(rng, dims, cuts, -0.22, 0.18) if cuts else 1.0
    values = jax.random.normal(rng, dims, jnp.float32) * deviation * level
    return jnp.minimum(jnp.maximum(values, -limit), limit).astype(kind)


def setup_inputs(seed: int = 0) -> dict:
    streams_of = jax.random.split(jax.random.key(seed), 14)
    return {
        "kv_cache": draw_kv_cache(jax.random.fold_in(streams_of[13], 71), 0),
        "lin_states": scatter_about(streams_of[1], (ROWS, HEADS_V, DK, DV), 1.0, 6.0, ((1, 4), (2, 32)), jnp.float32),
        "row_order": jax.random.permutation(streams_of[2], ROWS).astype(jnp.int32),
        "prompt_lengths": draw_prompt_lengths(jax.random.fold_in(streams_of[13], 71), 0),
        "att_query": draw_att_query(jax.random.fold_in(streams_of[13], 71), 0),
        "new_kv": scatter_about(streams_of[5], (ROWS, STEPS, FEAT), 1.0, 6.0, ((0, 32),)),
        "att_gate": scatter_about(streams_of[6], (ROWS, STEPS, HQ * HD), 1.0, 6.0, ((0, 32), (2, 4))),
        "lin_query": scatter_about(streams_of[7], (ROWS, STEPS, HEADS_K, DK), 1.0, 6.0, ((0, 32), (2, 4))),
        "lin_key": scatter_about(streams_of[8], (ROWS, STEPS, HEADS_K, DK), 1.0, 6.0, ((0, 32), (2, 4))),
        "lin_value": scatter_about(streams_of[9], (ROWS, STEPS, HEADS_V, DV), 1.0, 6.0, ((0, 32), (2, 4))),
        "lin_decay": jnp.clip(0.3 + 0.7 * jax.random.uniform(streams_of[10], (ROWS, STEPS, HEADS_V), jnp.float32) ** block_levels(streams_of[10], (ROWS, STEPS, HEADS_V), ((0, 32), (2, 4)), -0.2, 0.2), 0.3, 1.0),
        "lin_beta": jnp.clip(0.2 + 0.8 * jax.random.uniform(streams_of[11], (ROWS, STEPS, HEADS_V), jnp.float32) ** block_levels(streams_of[11], (ROWS, STEPS, HEADS_V), ((0, 32), (2, 4)), -0.2, 0.2), 0.2, 1.0),
        "lin_gate": scatter_about(streams_of[12], (ROWS, STEPS, HEADS_V, DV), 1.0, 6.0, ((0, 32), (2, 4))),
    }


def delta_rule(states, query, key, value, decay, beta, gate):
    ratio = value.shape[2] // query.shape[2]
    queries = jnp.repeat(query.astype(jnp.float32), ratio, axis=2)
    keyed = jnp.repeat(key.astype(jnp.float32), ratio, axis=2)
    queries = queries * lax.rsqrt(lax.optimization_barrier(jnp.sum(queries * queries, -1, keepdims=True)) + 1e-06) * queries.shape[-1] ** (-0.5)
    keyed = keyed * lax.rsqrt(lax.optimization_barrier(jnp.sum(keyed * keyed, -1, keepdims=True)) + 1e-06)
    outputs = []
    for step in range(value.shape[1]):
        key_now = keyed[:, step]
        rates = decay[:, step][..., None]
        strength = beta[:, step][..., None]
        recalled = jnp.einsum('rhk,rhkv->rhv', key_now, states, precision=lax.Precision.HIGHEST)
        change = strength * (value[:, step].astype(jnp.float32) - rates * recalled)
        states = rates[..., None] * states + key_now[..., None] * change[..., None, :]
        reading = jnp.einsum('rhk,rhkv->rhv', queries[:, step], states, precision=lax.Precision.HIGHEST)
        normed = reading * lax.rsqrt(lax.optimization_barrier(jnp.mean(reading * reading, -1, keepdims=True)) + 1e-06)
        outputs.append((normed * jax.nn.silu(gate[:, step].astype(jnp.float32))).astype(jnp.bfloat16))
    return (jnp.stack(outputs, axis=1), states)

def attend_row(cache_row, length, query, fresh):
    half = KVH * HD
    group = HQ // KVH
    scale = HD ** (-0.5)
    keys = cache_row[:, :half].reshape(LEN, KVH, HD).astype(jnp.float32)
    values = cache_row[:, half:].reshape(LEN, KVH, HD).astype(jnp.float32)
    fresh_keys = fresh[:, :half].reshape(STEPS, KVH, HD).astype(jnp.float32)
    fresh_values = fresh[:, half:].reshape(STEPS, KVH, HD).astype(jnp.float32)
    queries = query.reshape(STEPS, KVH, group, HD).astype(jnp.float32)
    cache_scores = jnp.einsum('sgjd,kgd->sgjk', queries, keys) * scale
    fresh_scores = jnp.einsum('sgjd,tgd->sgjt', queries, fresh_keys) * scale
    valid = (jnp.arange(LEN, dtype=jnp.int32) < length)[None, None, None, :]
    causal = (jnp.arange(STEPS)[None, :] <= jnp.arange(STEPS)[:, None])[:, None, None, :]
    cache_scores = jnp.where(valid, cache_scores, -1e+30)
    fresh_scores = jnp.where(causal, fresh_scores, -1e+30)
    top = jnp.maximum(lax.optimization_barrier(jnp.max(cache_scores, -1)), lax.optimization_barrier(jnp.max(fresh_scores, -1)))[..., None]
    cache_probs = jnp.where(valid, jnp.exp(cache_scores - top), 0.0)
    fresh_probs = jnp.where(causal, jnp.exp(fresh_scores - top), 0.0)
    total = lax.optimization_barrier(jnp.sum(cache_probs, -1)) + lax.optimization_barrier(jnp.sum(fresh_probs, -1))
    mixed = jnp.einsum('sgjk,kgd->sgjd', cache_probs.astype(jnp.bfloat16).astype(jnp.float32), values)
    mixed = mixed + jnp.einsum('sgjt,tgd->sgjd', fresh_probs.astype(jnp.bfloat16).astype(jnp.float32), fresh_values)
    return (mixed / total[..., None]).reshape(STEPS, HQ * HD)

def reference(kv_cache, lin_states, row_order, prompt_lengths, att_query, new_kv, att_gate, lin_query, lin_key, lin_value, lin_decay, lin_beta, lin_gate):
    lengths = prompt_lengths[row_order]

    def one_row(items):
        index, length, query, fresh = items
        cache_row = lax.dynamic_index_in_dim(kv_cache, index, 0, keepdims=False)
        return attend_row(cache_row, length, query, fresh)
    attended = lax.map(one_row, (row_order, lengths, att_query, new_kv))
    att_out = (attended * jax.nn.sigmoid(att_gate.astype(jnp.float32))).astype(jnp.bfloat16)
    states = lin_states[row_order]
    lin_out, final_states = delta_rule(states, lin_query, lin_key, lin_value, lin_decay, lin_beta, lin_gate)
    return (att_out, lin_out, final_states)
```

```python
import functools

import jax
import jax.numpy as jnp
from jax import lax
from jax.experimental import pallas as pl
from jax.experimental.pallas import tpu as pltpu
from jax.sharding import PartitionSpec as P

HQ = 16
KVH = 2
HD = 256
STEPS = 3
GROUP = HQ // KVH
QROWS = STEPS * GROUP
LANES = 128
NEGATIVE = -1e30

CHUNK = 8
CHUNKS = 4
PER_STEP = 4
NT = (((1,), (1,)), ((), ()))


def row_at(place, slot, other):
    core = (place[1] & 1) ^ other
    return 4 * ((place[1] >> 1) ^ (slot >> 1)) + 2 * core + (slot & 1)


def cache_spec(chunk, n, other, span):
    def at(step, order, lengths, place):
        return (order[row_at(place, chunk * CHUNK + step * PER_STEP + n, other)], 0, 0)

    return pl.BlockSpec((1, span, HD), at)


def gather_kernel(order, lengths, place, *refs):
    out = refs[-1]
    for n in range(PER_STEP):
        out[n] = refs[n][0]


def gather_rows(order, lengths, place, cache, first, count):
    span = cache.shape[1]
    return pl.pallas_call(
        gather_kernel,
        name="gather_rows",
        out_shape=jax.ShapeDtypeStruct((count * CHUNK, span, HD), cache.dtype),
        grid_spec=pltpu.PrefetchScalarGridSpec(
            num_scalar_prefetch=3,
            grid=(count * CHUNK // PER_STEP,),
            in_specs=[cache_spec(first, n, 1, span) for n in range(PER_STEP)],
            out_specs=pl.BlockSpec((PER_STEP, span, HD), lambda s, *_: (s, 0, 0)),
        ),
        cost_estimate=pl.CostEstimate(
            flops=0, bytes_accessed=2 * count * CHUNK * span * HD * 2, transcendentals=0
        ),
    )(order, lengths, place, *([cache] * PER_STEP))


def score_kernel(order, lengths, place, query, *refs, chunk):
    own, swapped, out = refs[:PER_STEP], refs[PER_STEP], refs[PER_STEP + 1]
    span = swapped.shape[1]
    step = pl.program_id(0)
    width = 2 * span
    tail = CHUNK * width

    @pl.when(step == 0)
    def _():
        out[:, tail:] = jnp.zeros((QROWS, LANES), out.dtype)

    @pl.when(place[0] < 2)
    def _():
        lane = lax.broadcasted_iota(jnp.int32, (QROWS, LANES), 1)
        column = lax.broadcasted_iota(jnp.int32, (QROWS, span), 1)
        position = jnp.concatenate(
            [column + place[1] * span, column + (place[1] ^ 1) * span], axis=1
        )
        extra = out[:, tail:].astype(jnp.float32)
        for n in range(PER_STEP):
            slot = step * PER_STEP + n
            length = lengths[order[row_at(place, chunk * CHUNK + slot, 0)]]
            q = query[n]
            scores = jnp.concatenate(
                [
                    lax.dot_general(q, own[n][0], NT, preferred_element_type=jnp.float32),
                    lax.dot_general(q, swapped[n], NT, preferred_element_type=jnp.float32),
                ],
                axis=1,
            ) * (HD ** (-0.5))
            valid = position < length
            scores = jnp.where(valid, scores, NEGATIVE)
            top = jnp.max(scores, axis=1, keepdims=True)
            top = top.astype(jnp.bfloat16).astype(jnp.float32)
            weights = jnp.where(valid, jnp.exp(scores - top), 0.0)
            total = jnp.sum(weights, axis=1, keepdims=True)
            coarse = total.astype(jnp.bfloat16).astype(jnp.float32)
            start = pl.multiple_of(slot * width, width)
            out[:, pl.ds(start, width)] = weights.astype(out.dtype)
            extra = jnp.where(lane == slot, top, extra)
            extra = jnp.where(lane == slot + CHUNK, coarse, extra)
            extra = jnp.where(lane == slot + 2 * CHUNK, total - coarse, extra)
        out[:, tail:] = extra.astype(out.dtype)


def score_rows(order, lengths, place, query, cache, swapped, chunk, swapped_at):
    span = cache.shape[1]
    steps = CHUNK // PER_STEP
    width = CHUNK * 2 * span + LANES
    return pl.pallas_call(
        functools.partial(score_kernel, chunk=chunk),
        name="score_rows",
        out_shape=jax.ShapeDtypeStruct((QROWS, width), jnp.bfloat16),
        grid_spec=pltpu.PrefetchScalarGridSpec(
            num_scalar_prefetch=3,
            grid=(steps,),
            in_specs=[pl.BlockSpec((PER_STEP, QROWS, HD), lambda s, *_: (s, 0, 0))]
            + [cache_spec(chunk, n, 0, span) for n in range(PER_STEP)]
            + [pl.BlockSpec((PER_STEP, span, HD), lambda s, *_: (swapped_at * steps + s, 0, 0))],
            out_specs=pl.BlockSpec((QROWS, width), lambda s, *_: (0, 0)),
        ),
        cost_estimate=pl.CostEstimate(
            flops=CHUNK * 4 * QROWS * span * HD,
            bytes_accessed=2 * CHUNK * span * HD * 2,
            transcendentals=CHUNK * QROWS * 2 * span,
        ),
    )(order, lengths, place, query, *([cache] * PER_STEP), swapped)


def mix_kernel(order, lengths, place, weights, *refs):
    own, swapped, out = refs[:PER_STEP], refs[PER_STEP], refs[-1]
    span = swapped.shape[1]
    step = pl.program_id(0)
    width = 2 * span
    tail = CHUNK * width

    @pl.when(place[0] >= 2)
    def _():
        extra = weights[:, tail:].astype(jnp.float32)
        for pair in range(PER_STEP // 2):
            rows = []
            for n in (2 * pair, 2 * pair + 1):
                slot = step * PER_STEP + n
                start = pl.multiple_of(slot * width, width)
                part = weights[:, pl.ds(start, width)]
                mixed = jnp.dot(
                    part[:, :span], own[n][0], preferred_element_type=jnp.float32
                ) + jnp.dot(part[:, span:], swapped[n], preferred_element_type=jnp.float32)
                mine = pltpu.roll(extra, (LANES - slot) % LANES, 1)
                rows.append(jnp.concatenate([mixed, mine], axis=1))
            chip = ((place[1] >> 1) & 1) ^ pair
            out[chip] = jnp.concatenate(rows, axis=0).astype(out.dtype)


def mix_rows(order, lengths, place, weights, cache, swapped, chunk, swapped_at, before):
    span = cache.shape[1]
    steps = CHUNK // PER_STEP
    chips = CHUNK * CHUNKS // 2
    width = HD + LANES

    def target(step, order, lengths, place):
        return ((place[1] >> 2) ^ (chunk * steps + step), 0, 0)

    in_specs = (
        [pl.BlockSpec(weights.shape, lambda s, *_: (0, 0))]
        + [cache_spec(chunk, n, 0, span) for n in range(PER_STEP)]
        + [pl.BlockSpec((PER_STEP, span, HD), lambda s, *_: (swapped_at * steps + s, 0, 0))]
    )
    operands = [order, lengths, place, weights, *([cache] * PER_STEP), swapped]
    aliases = {}
    if before is not None:
        in_specs.append(pl.BlockSpec(memory_space=pl.ANY))
        aliases = {len(operands): 0}
        operands.append(before)
    return pl.pallas_call(
        mix_kernel,
        name="mix_rows",
        out_shape=jax.ShapeDtypeStruct((chips, 2 * QROWS, width), jnp.bfloat16),
        grid_spec=pltpu.PrefetchScalarGridSpec(
            num_scalar_prefetch=3,
            grid=(steps,),
            in_specs=in_specs,
            out_specs=pl.BlockSpec((PER_STEP // 2, 2 * QROWS, width), target),
        ),
        input_output_aliases=aliases,
        cost_estimate=pl.CostEstimate(
            flops=CHUNK * 4 * QROWS * span * HD,
            bytes_accessed=2 * CHUNK * span * HD * 2,
            transcendentals=0,
        ),
    )(*operands)


def combine_kernel(place, parts, query, fresh, low, high):
    @pl.when(place[0] >= 2)
    def _():
        chips = parts.shape[0]
        second = place[0] & 1
        step = lax.broadcasted_iota(jnp.int32, (QROWS, STEPS), 0) // GROUP
        time = lax.broadcasted_iota(jnp.int32, (QROWS, STEPS), 1)
        keep = time <= step
        half = KVH * HD
        tops, totals = [], []
        for chip in range(chips):
            extra = parts[chip, :, HD:].astype(jnp.float32)
            tops.append(extra[:, 0:1])
            totals.append(extra[:, CHUNK : CHUNK + 1] + extra[:, 2 * CHUNK : 2 * CHUNK + 1])
        scores, values = [], []
        for row in range(2):
            news = fresh[row].astype(jnp.float32)
            keys = jnp.where(second == 1, news[:, HD:half], news[:, :HD])
            values.append(jnp.where(second == 1, news[:, half + HD :], news[:, half : half + HD]))
            q = query[row].astype(jnp.float32)
            columns = [
                jnp.sum(q * keys[t : t + 1], axis=1, keepdims=True) for t in range(STEPS)
            ]
            score = jnp.concatenate(columns, axis=1) * (HD ** (-0.5))
            scores.append(jnp.where(keep, score, NEGATIVE))
        score = jnp.concatenate(scores, axis=0)
        keep = jnp.concatenate([keep, keep], axis=0)
        top = jnp.max(score, axis=1, keepdims=True)
        for chip in range(chips):
            top = jnp.maximum(top, tops[chip])
        probs = jnp.where(keep, jnp.exp(score - top), 0.0)
        total = jnp.sum(probs, axis=1, keepdims=True)
        probs = probs.astype(jnp.bfloat16).astype(jnp.float32)
        mixed = []
        for row in range(2):
            mine = probs[row * QROWS : (row + 1) * QROWS]
            mixed.append(sum(mine[:, t : t + 1] * values[row][t : t + 1] for t in range(STEPS)))
        mixed = jnp.concatenate(mixed, axis=0)
        for chip in range(chips):
            factor = jnp.exp(tops[chip] - top)
            total = total + factor * totals[chip]
            mixed = mixed + factor * parts[chip, :, :HD].astype(jnp.float32)
        result = mixed / total
        heads = GROUP // 2
        for row in range(2):
            for s in range(STEPS):
                for a in range(heads):
                    at = row * QROWS + s * GROUP + a
                    low[row, s : s + 1, a * HD : (a + 1) * HD] = result[at : at + 1]
                    at = at + heads
                    high[row, s : s + 1, a * HD : (a + 1) * HD] = result[at : at + 1]


def combine(place, parts, query, fresh):
    heads = GROUP // 2
    shape = jax.ShapeDtypeStruct((2, STEPS, heads * HD), jnp.float32)
    whole = pl.BlockSpec(memory_space=pltpu.VMEM)
    return pl.pallas_call(
        combine_kernel,
        name="combine_parts",
        out_shape=(shape, shape),
        in_specs=[pl.BlockSpec(memory_space=pltpu.SMEM), whole, whole, whole],
        out_specs=(whole, whole),
        cost_estimate=pl.CostEstimate(
            flops=4 * parts.size, bytes_accessed=2 * parts.size, transcendentals=2000
        ),
    )(place, parts, query, fresh)


def delta_rule(states, query, key, value, decay, beta, gate):
    ratio = value.shape[2] // query.shape[2]
    queries = jnp.repeat(query.astype(jnp.float32), ratio, axis=2)
    keyed = jnp.repeat(key.astype(jnp.float32), ratio, axis=2)
    queries = (
        queries
        * lax.rsqrt(jnp.sum(queries * queries, -1, keepdims=True) + 1e-06)
        * queries.shape[-1] ** (-0.5)
    )
    keyed = keyed * lax.rsqrt(jnp.sum(keyed * keyed, -1, keepdims=True) + 1e-06)
    outputs = []
    for step in range(value.shape[1]):
        key_now = keyed[:, step]
        rates = decay[:, step][..., None]
        strength = beta[:, step][..., None]
        recalled = jnp.einsum("rhk,rhkv->rhv", key_now, states, precision=lax.Precision.HIGHEST)
        change = strength * (value[:, step].astype(jnp.float32) - rates * recalled)
        states = rates[..., None] * states + key_now[..., None] * change[..., None, :]
        reading = jnp.einsum(
            "rhk,rhkv->rhv", queries[:, step], states, precision=lax.Precision.HIGHEST
        )
        normed = reading * lax.rsqrt(jnp.mean(reading * reading, -1, keepdims=True) + 1e-06)
        outputs.append(
            (normed * jax.nn.silu(gate[:, step].astype(jnp.float32))).astype(jnp.bfloat16)
        )
    return (jnp.stack(outputs, axis=1), states)


def on_device(
    kv_cache,
    lin_states,
    row_order,
    prompt_lengths,
    att_query,
    new_kv,
    att_gate,
    lin_query,
    lin_key,
    lin_value,
    lin_decay,
    lin_beta,
    lin_gate,
):
    wide_count = lax.axis_size("wide")
    chips = wide_count // 2
    head_index = lax.axis_index("head")
    place = jnp.stack([head_index, lax.axis_index("wide")]).astype(jnp.int32)

    def across(array, distance):
        pairs = [(i, i ^ distance) for i in range(wide_count)]
        return lax.ppermute(array, "wide", pairs)

    query = lax.dynamic_slice_in_dim(att_query, (head_index % KVH) * GROUP, GROUP, 2)
    query = query.reshape(2, QROWS, HD)
    near = jnp.concatenate([query] + [across(query, 2 * t) for t in range(1, 4)], axis=0)

    first = across(gather_rows(row_order, prompt_lengths, place, kv_cache, 0, 1), 1)
    later = across(gather_rows(row_order, prompt_lengths, place, kv_cache, 1, 3), 1)
    swapped = [(first, 0), (later, 0), (later, 1), (later, 2)]

    asked = [near] + [across(near, 8 * u) for u in range(1, 4)]
    weights = []
    for chunk in range(CHUNKS):
        made = score_rows(
            row_order, prompt_lengths, place, asked[chunk], kv_cache,
            swapped[chunk][0], chunk, swapped[chunk][1],
        )
        weights.append(made)
    moved = [lax.ppermute(made, "head", [(0, 2), (1, 3)]) for made in weights]

    taken = lin_states.at[row_order].get(mode="promise_in_bounds", unique_indices=True)
    sent, _ = lax.optimization_barrier((taken.astype(jnp.bfloat16), weights[-1]))
    states = lax.all_to_all(sent, "wide", split_axis=0, concat_axis=2, tiled=True)

    payload = None
    for chunk in range(CHUNKS):
        payload = mix_rows(
            row_order, prompt_lengths, place, moved[chunk], kv_cache,
            swapped[chunk][0], chunk, swapped[chunk][1], payload,
        )
    same_core = [[2 * k + c for k in range(chips)] for c in range(2)]
    parts = lax.all_to_all(payload, "wide", 0, 0, tiled=True, axis_index_groups=same_core)
    low, high = combine(place, parts, query, new_kv)
    low_here = lax.ppermute(low, "head", [(2, 0), (3, 2)])
    high_here = lax.ppermute(high, "head", [(2, 1)])
    result = jnp.where(
        head_index == 3, high, jnp.where(head_index == 1, high_here, low_here)
    )
    att_out = (result * jax.nn.sigmoid(att_gate.astype(jnp.float32))).astype(jnp.bfloat16)

    lin_out, final_states = delta_rule(
        states.astype(jnp.float32), lin_query, lin_key, lin_value, lin_decay, lin_beta, lin_gate
    )
    return (att_out, lin_out, final_states)


def solution(mesh):
    placed = (
        P(None, "wide", "head"),
        P(None, "head", "wide", None),
        P(),
        P(),
        P("wide", None, None, None),
        P("wide", None, None),
        P("wide", None, "head"),
        P("wide", None, "head", None),
        P("wide", None, "head", None),
        P("wide", None, "head", None),
        P("wide", None, "head"),
        P("wide", None, "head"),
        P("wide", None, "head", None),
    )
    return jax.shard_map(
        on_device,
        mesh=mesh,
        in_specs=placed,
        out_specs=(
            P("wide", None, "head"),
            P("wide", None, "head", None),
            P("wide", "head", None, None),
        ),
        check_vma=False,
    )
```

```python
import functools

import jax
import jax.numpy as jnp
from jax import lax
from jax.experimental import pallas as pl
from jax.experimental.pallas import tpu as pltpu
from jax.sharding import PartitionSpec as P

HQ = 16
KVH = 2
HD = 256
STEPS = 3
GROUP = HQ // KVH
QROWS = STEPS * GROUP
LANES = 128
NEGATIVE = -1e30

CHUNK = 8
CHUNKS = 4
NT = (((1,), (1,)), ((), ()))
LIMIT = 16 * 2**20
VMEM = pl.BlockSpec(memory_space=pltpu.VMEM)
SMEM = pl.BlockSpec(memory_space=pltpu.SMEM)
ANY = pl.BlockSpec(memory_space=pltpu.HBM)
PARAMS = pltpu.CompilerParams(vmem_limit_bytes=LIMIT)
FREE = pl.CostEstimate(flops=0, bytes_accessed=0, transcendentals=0)

ROWS = 64
PLACE = 2 * ROWS


def near(array):
    return pltpu.with_memory_space_constraint(array, pltpu.VMEM)


def far(array):
    return pltpu.with_memory_space_constraint(array, pltpu.HBM)


def prefill_row(info, slot, other=0):
    core = (info[PLACE + 1] & 1) ^ other
    return info[4 * (slot // 2) + 2 * core + slot % 2]


def gather_kernel(info, cache, *refs, first):
    outs, (held, arrived, left) = refs[:-3], refs[-3:]
    size = outs[0].shape[0]
    count = held.shape[0]
    reads = [
        pltpu.make_async_copy(cache.at[prefill_row(info, first + n, 1)], held.at[n], arrived.at[n])
        for n in range(count)
    ]
    writes = [
        pltpu.make_async_copy(held.at[n], outs[n // size].at[n % size], left.at[n])
        for n in range(count)
    ]
    for read in reads:
        read.start()
    for read, write in zip(reads, writes):
        read.wait()
        write.start()
    for write in writes:
        write.wait()


def gather_rows(info, cache, first, count, parts):
    span, dtype = cache.shape[1], cache.dtype
    copies = pltpu.SemaphoreType.DMA((count,))
    return pl.pallas_call(
        functools.partial(gather_kernel, first=first),
        name="gather_rows",
        out_shape=[pltpu.HBM((count // parts, span, HD), dtype)] * parts,
        in_specs=[SMEM, ANY],
        out_specs=[ANY] * parts,
        scratch_shapes=[pltpu.VMEM((count, span, HD), dtype), copies, copies],
        compiler_params=PARAMS,
        cost_estimate=FREE,
    )(info, far(cache))


def hold_kernel(array, out):
    pass


def hold(array, cost):
    return pl.pallas_call(
        hold_kernel,
        name="hold",
        out_shape=pltpu.VMEM(array.shape, array.dtype),
        in_specs=[VMEM],
        out_specs=VMEM,
        input_output_aliases={0: 0},
        compiler_params=PARAMS,
        cost_estimate=pl.CostEstimate(flops=cost, bytes_accessed=0, transcendentals=0),
    )(near(array))


def fetches(info, cache, swapped, own, other, arrived, chunk):
    copies = [
        pltpu.make_async_copy(
            cache.at[prefill_row(info, chunk * CHUNK + n)], own.at[n], arrived.at[n]
        )
        for n in range(CHUNK)
    ]
    if swapped is not None:
        copies.append(pltpu.make_async_copy(swapped, other, arrived.at[CHUNK]))
    return copies


def start(copies):
    for copy in copies:
        copy.start()


def wait(copies):
    for copy in copies:
        copy.wait()


ARRIVED = pltpu.SemaphoreType.DMA((CHUNK + 1,))


def load_kernel(info, cache, own, arrived, *, chunk):
    copies = fetches(info, cache, None, own, None, arrived, chunk)
    start(copies)
    wait(copies)


def load_rows(info, cache, chunk):
    return pl.pallas_call(
        functools.partial(load_kernel, chunk=chunk),
        name="load_rows",
        out_shape=pltpu.VMEM((CHUNK, *cache.shape[1:]), cache.dtype),
        in_specs=[SMEM, ANY],
        out_specs=VMEM,
        scratch_shapes=[ARRIVED],
        compiler_params=PARAMS,
        cost_estimate=FREE,
    )(info, far(cache))


def score_kernel(info, query, own, other, *refs, chunk):
    if chunk + 1 < CHUNKS:
        cache, swapped, out, own_next, other_next, arrived = refs
    else:
        (out,) = refs
    span = own.shape[1]
    width = 2 * span

    @pl.when(info[PLACE] < 2)
    def _():
        if chunk + 1 < CHUNKS:
            copies = fetches(info, cache, swapped, own_next, other_next, arrived, chunk + 1)
            start(copies)
        lane = lax.broadcasted_iota(jnp.int32, (QROWS, LANES), 1)
        column = lax.broadcasted_iota(jnp.int32, (QROWS, span), 1)
        wide = info[PLACE + 1]
        position = jnp.concatenate([column + wide * span, column + (wide ^ 1) * span], axis=1)
        extra = jnp.zeros((QROWS, LANES), jnp.float32)
        for n in range(CHUNK):
            slot = chunk * CHUNK + n
            q = query[slot]
            scores = jnp.concatenate(
                [
                    lax.dot_general(q, own[n], NT, preferred_element_type=jnp.float32),
                    lax.dot_general(q, other[n], NT, preferred_element_type=jnp.float32),
                ],
                axis=1,
            ) * (HD ** (-0.5))
            valid = position < info[ROWS + prefill_row(info, slot)]
            scores = jnp.where(valid, scores, NEGATIVE)
            top = jnp.max(scores, axis=1, keepdims=True)
            top = top.astype(jnp.bfloat16).astype(jnp.float32)
            weights = jnp.where(valid, jnp.exp(scores - top), 0.0)
            total = jnp.sum(weights, axis=1, keepdims=True)
            coarse = total.astype(jnp.bfloat16).astype(jnp.float32)
            out[:, n * width : (n + 1) * width] = weights.astype(out.dtype)
            extra = jnp.where(lane == n, top, extra)
            extra = jnp.where(lane == n + CHUNK, coarse, extra)
            extra = jnp.where(lane == n + 2 * CHUNK, total - coarse, extra)
        out[:, CHUNK * width :] = extra.astype(out.dtype)
        if chunk + 1 < CHUNKS:
            wait(copies)


def score_rows(info, query, own, other, cache, swapped, chunk):
    span, dtype = cache.shape[1], cache.dtype
    last = chunk + 1 == CHUNKS
    rows = pltpu.VMEM((CHUNK, span, HD), dtype)
    made = pl.pallas_call(
        functools.partial(score_kernel, chunk=chunk),
        name="score_rows",
        out_shape=[pltpu.VMEM((QROWS, CHUNK * 2 * span + LANES), jnp.bfloat16)]
        + ([] if last else [rows, rows]),
        in_specs=[SMEM, VMEM, VMEM, VMEM] + ([] if last else [ANY, ANY]),
        out_specs=[VMEM] if last else [VMEM] * 3,
        scratch_shapes=[] if last else [ARRIVED],
        compiler_params=PARAMS,
        cost_estimate=FREE,
    )(
        info, near(query), near(own), near(other),
        *(() if last else (far(cache), far(swapped))),
    )
    return (made[0], None, None) if last else made


LINES = 2 * QROWS
SLAB = 2 * LINES + 16
EXTRAS = 8


def mix_kernel(info, weights, *refs, chunk):
    last = chunk + 1 == CHUNKS
    fetch_last = chunk + 2 == CHUNKS
    made, left = refs[-2:]
    if last:
        own, other, _, out = refs[:4]
    elif fetch_last:
        cache, swapped, swapped_last, _, out, own_last, other_last = refs[:7]
        own, other, arrived, arrived_last = refs[7:11]
    else:
        cache, swapped = refs[:2]
        out, own, other, arrived = refs[-6:-2]
    span = own.shape[1]
    width = 2 * span

    @pl.when(info[PLACE] >= 2)
    def _():
        if not last:
            copies = fetches(info, cache, swapped, own, other, arrived, chunk)
            start(copies)
        if fetch_last:
            copies_last = fetches(
                info, cache, swapped_last, own_last, other_last, arrived_last, chunk + 1
            )
            start(copies_last)
        extra = weights[:, CHUNK * width :].astype(jnp.float32)
        extra = jnp.concatenate([extra, jnp.zeros((LANES - QROWS, LANES), jnp.float32)], axis=0)
        extra = jnp.transpose(extra)
        blank = jnp.zeros((16 - 6, LANES), jnp.float32)
        if not last:
            wait(copies)
        for pair in range(CHUNK // 2):
            rows, lines = [], []
            for n in (2 * pair, 2 * pair + 1):
                at = n * width
                rows.append(
                    jnp.dot(
                        weights[:, at : at + span], own[n], preferred_element_type=jnp.float32
                    )
                    + jnp.dot(
                        weights[:, at + span : at + width],
                        other[n],
                        preferred_element_type=jnp.float32,
                    )
                )
                lines += [extra[n + k * CHUNK : n + k * CHUNK + 1] for k in range(3)]
            slab = [row[:, :LANES] for row in rows] + [row[:, LANES:] for row in rows]
            made[pair] = jnp.concatenate([*slab, *lines, blank], axis=0).astype(made.dtype)
        copy = pltpu.make_async_copy(
            made, out.at[pl.ds(chunk * CHUNK // 2, CHUNK // 2)], left.at[0]
        )
        copy.start()
        copy.wait()
        if fetch_last:
            wait(copies_last)


def mix_rows(info, weights, cache, swapped, chunk, before, rows, cost):
    last = chunk + 1 == CHUNKS
    fetch_last = chunk + 2 == CHUNKS
    held = pltpu.VMEM((CHUNK, *cache.shape[1:]), cache.dtype)
    payload = pltpu.HBM((CHUNK * CHUNKS // 2, SLAB, LANES), jnp.bfloat16)
    if last:
        in_specs = [SMEM, VMEM, VMEM, VMEM]
        operands = [info, near(weights), near(rows[0]), near(rows[1])]
    else:
        in_specs = [SMEM, VMEM, ANY, ANY]
        operands = [info, near(weights), far(cache), far(swapped[chunk])]
    if fetch_last:
        in_specs.append(ANY)
        operands.append(far(swapped[chunk + 1]))
    aliases = {}
    if before is not None:
        in_specs.append(ANY)
        aliases = {len(operands): 0}
        operands.append(far(before))
    made = pl.pallas_call(
        functools.partial(mix_kernel, chunk=chunk),
        name="mix_rows",
        out_shape=[payload] + ([held, held] if fetch_last else []),
        in_specs=in_specs,
        out_specs=[ANY] + ([VMEM, VMEM] if fetch_last else []),
        input_output_aliases=aliases,
        scratch_shapes=([] if last else [held, held, ARRIVED])
        + ([ARRIVED] if fetch_last else [])
        + [pltpu.VMEM((CHUNK // 2, SLAB, LANES), jnp.bfloat16), pltpu.SemaphoreType.DMA((1,))],
        compiler_params=PARAMS,
        cost_estimate=pl.CostEstimate(flops=cost, bytes_accessed=0, transcendentals=0),
    )(*operands)
    return made[0], made[1:]


def combine_kernel(info, parts, query, fresh, low, high):
    @pl.when(info[PLACE] >= 2)
    def _():
        chips = parts.shape[0]
        second = info[PLACE] & 1
        step = lax.broadcasted_iota(jnp.int32, (QROWS, STEPS), 0) // GROUP
        time = lax.broadcasted_iota(jnp.int32, (QROWS, STEPS), 1)
        keep = time <= step
        half = KVH * HD
        extras = [parts[chip, 2 * LINES :].astype(jnp.float32)[:EXTRAS] for chip in range(chips)]
        extras = jnp.transpose(jnp.concatenate(extras, axis=0))

        def line(chip, which):
            at = chip * EXTRAS + which
            return jnp.concatenate(
                [extras[:QROWS, at : at + 1], extras[:QROWS, at + 3 : at + 4]], axis=0
            )

        tops = [line(chip, 0) for chip in range(chips)]
        totals = [line(chip, 1) + line(chip, 2) for chip in range(chips)]
        scores, values = [], []
        for row in range(2):
            news = fresh[row].astype(jnp.float32)
            keys = jnp.where(second == 1, news[:, HD:half], news[:, :HD])
            values.append(jnp.where(second == 1, news[:, half + HD :], news[:, half : half + HD]))
            q = jnp.where(second == 1, query[row, :, GROUP:], query[row, :, :GROUP])
            q = q.reshape(QROWS, HD).astype(jnp.float32)
            columns = [
                jnp.sum(q * keys[t : t + 1], axis=1, keepdims=True) for t in range(STEPS)
            ]
            score = jnp.concatenate(columns, axis=1) * (HD ** (-0.5))
            scores.append(jnp.where(keep, score, NEGATIVE))
        score = jnp.concatenate(scores, axis=0)
        keep = jnp.concatenate([keep, keep], axis=0)
        top = jnp.max(score, axis=1, keepdims=True)
        for chip in range(chips):
            top = jnp.maximum(top, tops[chip])
        probs = jnp.where(keep, jnp.exp(score - top), 0.0)
        total = jnp.sum(probs, axis=1, keepdims=True)
        probs = probs.astype(jnp.bfloat16).astype(jnp.float32)
        mixed = []
        for row in range(2):
            mine = probs[row * QROWS : (row + 1) * QROWS]
            mixed.append(sum(mine[:, t : t + 1] * values[row][t : t + 1] for t in range(STEPS)))
        mixed = jnp.concatenate(mixed, axis=0)
        halves = [mixed[:, :LANES], mixed[:, LANES:]]
        for chip in range(chips):
            factor = jnp.exp(tops[chip] - top)
            total = total + factor * totals[chip]
            for k in range(2):
                part = parts[chip, k * LINES : (k + 1) * LINES].astype(jnp.float32)
                halves[k] = halves[k] + factor * part
        result = jnp.concatenate(halves, axis=1) / total
        heads = GROUP // 2
        for row in range(2):
            for s in range(STEPS):
                for a in range(heads):
                    at = row * QROWS + s * GROUP + a
                    low[row, s : s + 1, a * HD : (a + 1) * HD] = result[at : at + 1]
                    at = at + heads
                    high[row, s : s + 1, a * HD : (a + 1) * HD] = result[at : at + 1]


def combine(info, parts, query, fresh):
    heads = GROUP // 2
    shape = pltpu.VMEM((2, STEPS, heads * HD), jnp.float32)
    return pl.pallas_call(
        combine_kernel,
        name="combine_parts",
        out_shape=(shape, shape),
        in_specs=[SMEM, VMEM, VMEM, VMEM],
        out_specs=(VMEM, VMEM),
        compiler_params=PARAMS,
        cost_estimate=FREE,
    )(info, near(parts), near(query), near(fresh))


def delta_kernel(decay, beta, states, query, key, value, gate, out, final, rows):
    batch, steps, heads_k, width = key.shape
    heads_v = value.shape[2]
    ratio = heads_v // heads_k
    keys_at = batch * steps * heads_k

    def column(row, step, head):
        return (row * steps + step) * heads_k + head

    rows[...] = jnp.zeros_like(rows)
    for row in range(batch):
        for step in range(steps):
            at = column(row, step, 0)
            q = query[row, step].astype(jnp.float32)
            k = key[row, step].astype(jnp.float32)
            q = q * lax.rsqrt(jnp.sum(q * q, -1, keepdims=True) + 1e-06) * width ** (-0.5)
            k = k * lax.rsqrt(jnp.sum(k * k, -1, keepdims=True) + 1e-06)
            rows[at : at + heads_k] = q
            rows[keys_at + at : keys_at + at + heads_k] = k
    columns = jnp.transpose(rows[...])
    for row in range(batch):
        made = [[] for _ in range(steps)]
        values = [value[row, step].astype(jnp.float32) for step in range(steps)]
        for head in range(heads_v):
            state = states[row, head].astype(jnp.float32)
            for step in range(steps):
                at = column(row, step, head // ratio)
                q = columns[:, at : at + 1]
                k = columns[:, keys_at + at : keys_at + at + 1]
                rate = decay[row, step, head]
                recalled = jnp.sum(k * state, axis=0, keepdims=True)
                change = beta[row, step, head] * (values[step][head : head + 1] - rate * recalled)
                state = rate * state + k * change
                made[step].append(jnp.sum(q * state, axis=0, keepdims=True))
            final[row, head] = state
        for step in range(steps):
            read = jnp.concatenate(made[step], axis=0)
            read = read * lax.rsqrt(jnp.mean(read * read, -1, keepdims=True) + 1e-06)
            level = gate[row, step].astype(jnp.float32)
            out[row, step] = (read * (level * jax.nn.sigmoid(level))).astype(out.dtype)


def delta_rule(states, query, key, value, decay, beta, gate):
    width = key.shape[-1]
    return pl.pallas_call(
        delta_kernel,
        name="delta_rule",
        out_shape=(
            jax.ShapeDtypeStruct(value.shape, jnp.bfloat16),
            jax.ShapeDtypeStruct(states.shape, jnp.float32),
        ),
        in_specs=[SMEM, SMEM] + [VMEM] * 5,
        out_specs=(VMEM, VMEM),
        scratch_shapes=[pltpu.VMEM((width, width), jnp.float32)],
        compiler_params=PARAMS,
        cost_estimate=FREE,
    )(decay, beta, states, query, key, value, gate)


def on_device(
    kv_cache,
    lin_states,
    row_order,
    prompt_lengths,
    att_query,
    new_kv,
    att_gate,
    lin_query,
    lin_key,
    lin_value,
    lin_decay,
    lin_beta,
    lin_gate,
):
    wide_count = lax.axis_size("wide")
    chips = wide_count // 2
    head_index = lax.axis_index("head")
    place = jnp.stack([head_index, lax.axis_index("wide")]).astype(jnp.int32)
    info = jnp.concatenate([row_order, prompt_lengths, place])

    def across(array):
        pairs = [(i, i ^ 1) for i in range(wide_count)]
        return lax.ppermute(array, "wide", pairs)

    def after(array, *others):
        return lax.optimization_barrier((array, *others))[0]

    same_core = [[2 * k + c for k in range(chips)] for c in range(2)]

    def between_chips(array):
        return lax.all_to_all(array, "wide", 0, 0, tiled=True, axis_index_groups=same_core)

    mine = lax.dynamic_slice_in_dim(att_query, (head_index % KVH) * GROUP, GROUP, 2)
    copies = jnp.broadcast_to(mine.reshape(1, 2, QROWS, HD), (chips, 2, QROWS, HD))
    query = hold(between_chips(copies.reshape(2 * chips, QROWS, HD)), 30 * 10**9)

    taken = lin_states.at[row_order].get(mode="promise_in_bounds", unique_indices=True)
    taken = taken.astype(jnp.bfloat16)
    made = gather_rows(info, kv_cache, 0, CHUNK, 1)
    made += gather_rows(
        after(info, taken, *made), kv_cache, CHUNK, CHUNK * (CHUNKS - 1), CHUNKS - 1
    )
    swapped = [across(part) for part in made]

    weights = []
    own, other = load_rows(after(info, *made), kv_cache, 0), swapped[0]
    for chunk in range(CHUNKS):
        following = swapped[min(chunk + 1, CHUNKS - 1)]
        made, own, other = score_rows(info, query, own, other, kv_cache, following, chunk)
        weights.append(made)
    moved = [lax.ppermute(made, "head", [(0, 2), (1, 3)]) for made in weights]

    states = lax.all_to_all(
        after(taken, weights[-1]), "wide", split_axis=0, concat_axis=2, tiled=True
    )

    payload, rows = None, None
    for chunk in range(CHUNKS):
        cost = 10 * 10**9 if chunk == CHUNKS - 1 else 100 * 10**6
        payload, rows = mix_rows(
            info, moved[chunk], kv_cache, swapped, chunk, payload, rows, cost
        )
    parts = between_chips(payload)
    lin_out, final_states = delta_rule(
        after(states, payload), lin_query, lin_key, lin_value, lin_decay, lin_beta, lin_gate
    )
    low, high = combine(info, parts, att_query, after(new_kv, lin_out))
    low_here = lax.ppermute(low, "head", [(2, 0), (3, 2)])
    high_here = lax.ppermute(high, "head", [(2, 1)])
    result = jnp.where(
        head_index == 3, high, jnp.where(head_index == 1, high_here, low_here)
    )
    att_out = (result * jax.nn.sigmoid(att_gate.astype(jnp.float32))).astype(jnp.bfloat16)

    return (att_out, lin_out, final_states)


def solution(mesh):
    placed = (
        P(None, "wide", "head"),
        P(None, "head", "wide", None),
        P(),
        P(),
        P("wide", None, None, None),
        P("wide", None, None),
        P("wide", None, "head"),
        P("wide", None, "head", None),
        P("wide", None, "head", None),
        P("wide", None, "head", None),
        P("wide", None, "head"),
        P("wide", None, "head"),
        P("wide", None, "head", None),
    )
    return jax.shard_map(
        on_device,
        mesh=mesh,
        in_specs=placed,
        out_specs=(
            P("wide", None, "head"),
            P("wide", None, "head", None),
            P("wide", "head", None, None),
        ),
        check_vma=False,
    )
```

```python
import functools

import jax
import jax.numpy as jnp
from jax import lax
from jax.experimental import pallas as pl
from jax.experimental.pallas import tpu as pltpu
from jax.sharding import PartitionSpec as P

HQ = 16
KVH = 2
HD = 256
STEPS = 3
GROUP = HQ // KVH
QROWS = STEPS * GROUP
LANES = 128
NEGATIVE = -1e30

CHUNK = 16
CHUNKS = 2
GROUP_ROWS = 4
NT = (((1,), (1,)), ((), ()))
LIMIT = 16 * 2**20
VMEM = pl.BlockSpec(memory_space=pltpu.VMEM)
SMEM = pl.BlockSpec(memory_space=pltpu.SMEM)
ANY = pl.BlockSpec(memory_space=pltpu.HBM)
PARAMS = pltpu.CompilerParams(vmem_limit_bytes=LIMIT)
FREE = pl.CostEstimate(flops=0, bytes_accessed=0, transcendentals=0)

ROWS = 64
PLACE = 2 * ROWS


def near(array):
    return pltpu.with_memory_space_constraint(array, pltpu.VMEM)


def far(array):
    return pltpu.with_memory_space_constraint(array, pltpu.HBM)


def prefill_row(info, slot, other=0):
    core = (info[PLACE + 1] & 1) ^ other
    return info[4 * (slot // 2) + 2 * core + slot % 2]


def gather_kernel(info, cache, *refs, first):
    outs, (held, arrived, left) = refs[:-3], refs[-3:]
    size = outs[0].shape[0]
    count = held.shape[0]
    reads = [
        pltpu.make_async_copy(cache.at[prefill_row(info, first + n, 1)], held.at[n], arrived.at[n])
        for n in range(count)
    ]
    writes = [
        pltpu.make_async_copy(held.at[n], outs[n // size].at[n % size], left.at[n])
        for n in range(count)
    ]
    for read in reads:
        read.start()
    for read, write in zip(reads, writes):
        read.wait()
        write.start()
    for write in writes:
        write.wait()


def gather_rows(info, cache, first, count, parts):
    span, dtype = cache.shape[1], cache.dtype
    copies = pltpu.SemaphoreType.DMA((count,))
    return pl.pallas_call(
        functools.partial(gather_kernel, first=first),
        name="gather_rows",
        out_shape=[pltpu.HBM((count // parts, span, HD), dtype)] * parts,
        in_specs=[SMEM, ANY],
        out_specs=[ANY] * parts,
        scratch_shapes=[pltpu.VMEM((count, span, HD), dtype), copies, copies],
        compiler_params=PARAMS,
        cost_estimate=FREE,
    )(info, far(cache))


def hold_kernel(array, out):
    pass


def hold(array, cost):
    return pl.pallas_call(
        hold_kernel,
        name="hold",
        out_shape=pltpu.VMEM(array.shape, array.dtype),
        in_specs=[VMEM],
        out_specs=VMEM,
        input_output_aliases={0: 0},
        compiler_params=PARAMS,
        cost_estimate=pl.CostEstimate(flops=cost, bytes_accessed=0, transcendentals=0),
    )(near(array))


def fetches(info, cache, swapped, own, other, arrived, chunk):
    groups = []
    for first in range(0, CHUNK, GROUP_ROWS):
        copies = [
            pltpu.make_async_copy(
                cache.at[prefill_row(info, chunk * CHUNK + n)], own.at[n], arrived.at[n]
            )
            for n in range(first, first + GROUP_ROWS)
        ]
        span = pl.ds(first, GROUP_ROWS)
        copies.append(
            pltpu.make_async_copy(
                swapped.at[span], other.at[span], arrived.at[CHUNK + first // GROUP_ROWS]
            )
        )
        groups.append(copies)
    return groups


def start(groups):
    for copies in groups:
        for copy in copies:
            copy.start()


def wait(groups):
    for copies in groups:
        for copy in copies:
            copy.wait()


ARRIVED = pltpu.SemaphoreType.DMA((CHUNK + CHUNK // GROUP_ROWS,))


def score_kernel(info, query, cache, swapped, out, own, other, arrived, *, chunk):
    span = own.shape[1]
    width = 2 * span

    @pl.when(info[PLACE] < 2)
    def _():
        groups = fetches(info, cache, swapped, own, other, arrived, chunk)
        start(groups)
        lane = lax.broadcasted_iota(jnp.int32, (QROWS, LANES), 1)
        column = lax.broadcasted_iota(jnp.int32, (QROWS, span), 1)
        wide = info[PLACE + 1]
        position = jnp.concatenate([column + wide * span, column + (wide ^ 1) * span], axis=1)
        extra = jnp.zeros((QROWS, LANES), jnp.float32)
        for n in range(CHUNK):
            if n % GROUP_ROWS == 0:
                wait(groups[n // GROUP_ROWS : n // GROUP_ROWS + 1])
            slot = chunk * CHUNK + n
            q = query[slot]
            scores = jnp.concatenate(
                [
                    lax.dot_general(q, own[n], NT, preferred_element_type=jnp.float32),
                    lax.dot_general(q, other[n], NT, preferred_element_type=jnp.float32),
                ],
                axis=1,
            ) * (HD ** (-0.5))
            valid = position < info[ROWS + prefill_row(info, slot)]
            scores = jnp.where(valid, scores, NEGATIVE)
            top = jnp.max(scores, axis=1, keepdims=True)
            top = top.astype(jnp.bfloat16).astype(jnp.float32)
            weights = jnp.where(valid, jnp.exp(scores - top), 0.0)
            total = jnp.sum(weights, axis=1, keepdims=True)
            coarse = total.astype(jnp.bfloat16).astype(jnp.float32)
            out[:, n * width : (n + 1) * width] = weights.astype(out.dtype)
            extra = jnp.where(lane == n, top, extra)
            extra = jnp.where(lane == n + CHUNK, coarse, extra)
            extra = jnp.where(lane == n + 2 * CHUNK, total - coarse, extra)
        out[:, CHUNK * width :] = extra.astype(out.dtype)


def held_rows(cache):
    return pltpu.VMEM((CHUNK, *cache.shape[1:]), cache.dtype)


def score_rows(info, query, cache, swapped, chunk):
    width = CHUNK * 2 * cache.shape[1] + LANES
    return pl.pallas_call(
        functools.partial(score_kernel, chunk=chunk),
        name="score_rows",
        out_shape=pltpu.VMEM((QROWS, width), jnp.bfloat16),
        in_specs=[SMEM, VMEM, ANY, ANY],
        out_specs=VMEM,
        scratch_shapes=[held_rows(cache), held_rows(cache), ARRIVED],
        compiler_params=PARAMS,
        cost_estimate=FREE,
    )(info, near(query), far(cache), far(swapped))


LINES = 2 * QROWS
SLAB = 2 * LINES + 16
EXTRAS = 8


def mix_kernel(info, weights, *refs, chunk):
    last = chunk + 1 == CHUNKS
    fetch_last = chunk + 2 == CHUNKS
    made, left = refs[-2:]
    if last:
        own, other = refs[:2]
        out = refs[-3]
    elif fetch_last:
        cache, swapped, swapped_last = refs[:3]
        out, own_last, other_last, own, other, arrived, arrived_last = refs[-9:-2]
    else:
        cache, swapped = refs[:2]
        out, own, other, arrived = refs[-6:-2]
    span = own.shape[1]
    width = 2 * span

    @pl.when(info[PLACE] >= 2)
    def _():
        if not last:
            copies = fetches(info, cache, swapped, own, other, arrived, chunk)
            start(copies)
        if fetch_last:
            copies_last = fetches(
                info, cache, swapped_last, own_last, other_last, arrived_last, chunk + 1
            )
            start(copies_last)
        extra = weights[:, CHUNK * width :].astype(jnp.float32)
        extra = jnp.concatenate([extra, jnp.zeros((LANES - QROWS, LANES), jnp.float32)], axis=0)
        extra = jnp.transpose(extra)
        blank = jnp.zeros((16 - 6, LANES), jnp.float32)
        for pair in range(CHUNK // 2):
            if not last and (2 * pair) % GROUP_ROWS == 0:
                wait(copies[2 * pair // GROUP_ROWS : 2 * pair // GROUP_ROWS + 1])
            rows, lines = [], []
            for n in (2 * pair, 2 * pair + 1):
                at = n * width
                rows.append(
                    jnp.dot(
                        weights[:, at : at + span], own[n], preferred_element_type=jnp.float32
                    )
                    + jnp.dot(
                        weights[:, at + span : at + width],
                        other[n],
                        preferred_element_type=jnp.float32,
                    )
                )
                lines += [extra[n + k * CHUNK : n + k * CHUNK + 1] for k in range(3)]
            slab = [row[:, :LANES] for row in rows] + [row[:, LANES:] for row in rows]
            made[pair] = jnp.concatenate([*slab, *lines, blank], axis=0).astype(made.dtype)
        copy = pltpu.make_async_copy(
            made, out.at[pl.ds(chunk * CHUNK // 2, CHUNK // 2)], left.at[0]
        )
        copy.start()
        copy.wait()
        if fetch_last:
            wait(copies_last)


def mix_rows(info, weights, cache, swapped, chunk, before, rows, cost):
    last = chunk + 1 == CHUNKS
    fetch_last = chunk + 2 == CHUNKS
    held = held_rows(cache)
    payload = pltpu.HBM((CHUNK * CHUNKS // 2, SLAB, LANES), jnp.bfloat16)
    if last:
        in_specs = [SMEM, VMEM, VMEM, VMEM]
        operands = [info, near(weights), near(rows[0]), near(rows[1])]
    else:
        in_specs = [SMEM, VMEM, ANY, ANY]
        operands = [info, near(weights), far(cache), far(swapped[chunk])]
    if fetch_last:
        in_specs.append(ANY)
        operands.append(far(swapped[chunk + 1]))
    aliases = {}
    if before is not None:
        in_specs.append(ANY)
        aliases = {len(operands): 0}
        operands.append(far(before))
    made = pl.pallas_call(
        functools.partial(mix_kernel, chunk=chunk),
        name="mix_rows",
        out_shape=[payload] + ([held, held] if fetch_last else []),
        in_specs=in_specs,
        out_specs=[ANY] + ([VMEM, VMEM] if fetch_last else []),
        input_output_aliases=aliases,
        scratch_shapes=([] if last else [held, held, ARRIVED])
        + ([ARRIVED] if fetch_last else [])
        + [pltpu.VMEM((CHUNK // 2, SLAB, LANES), jnp.bfloat16), pltpu.SemaphoreType.DMA((1,))],
        compiler_params=PARAMS,
        cost_estimate=pl.CostEstimate(flops=cost, bytes_accessed=0, transcendentals=0),
    )(*operands)
    return made[0], made[1:]


def combine_kernel(info, parts, query, fresh, low, high):
    @pl.when(info[PLACE] >= 2)
    def _():
        chips = parts.shape[0]
        second = info[PLACE] & 1
        step = lax.broadcasted_iota(jnp.int32, (QROWS, STEPS), 0) // GROUP
        time = lax.broadcasted_iota(jnp.int32, (QROWS, STEPS), 1)
        keep = time <= step
        half = KVH * HD
        extras = [parts[chip, 2 * LINES :].astype(jnp.float32)[:EXTRAS] for chip in range(chips)]
        extras = jnp.transpose(jnp.concatenate(extras, axis=0))

        def line(chip, which):
            at = chip * EXTRAS + which
            return jnp.concatenate(
                [extras[:QROWS, at : at + 1], extras[:QROWS, at + 3 : at + 4]], axis=0
            )

        tops = [line(chip, 0) for chip in range(chips)]
        totals = [line(chip, 1) + line(chip, 2) for chip in range(chips)]
        scores, values = [], []
        for row in range(2):
            news = fresh[row].astype(jnp.float32)
            keys = jnp.where(second == 1, news[:, HD:half], news[:, :HD])
            values.append(jnp.where(second == 1, news[:, half + HD :], news[:, half : half + HD]))
            q = jnp.where(second == 1, query[row, :, GROUP:], query[row, :, :GROUP])
            q = q.reshape(QROWS, HD).astype(jnp.float32)
            columns = [
                jnp.sum(q * keys[t : t + 1], axis=1, keepdims=True) for t in range(STEPS)
            ]
            score = jnp.concatenate(columns, axis=1) * (HD ** (-0.5))
            scores.append(jnp.where(keep, score, NEGATIVE))
        score = jnp.concatenate(scores, axis=0)
        keep = jnp.concatenate([keep, keep], axis=0)
        top = jnp.max(score, axis=1, keepdims=True)
        for chip in range(chips):
            top = jnp.maximum(top, tops[chip])
        probs = jnp.where(keep, jnp.exp(score - top), 0.0)
        total = jnp.sum(probs, axis=1, keepdims=True)
        probs = probs.astype(jnp.bfloat16).astype(jnp.float32)
        mixed = []
        for row in range(2):
            mine = probs[row * QROWS : (row + 1) * QROWS]
            mixed.append(sum(mine[:, t : t + 1] * values[row][t : t + 1] for t in range(STEPS)))
        mixed = jnp.concatenate(mixed, axis=0)
        halves = [mixed[:, :LANES], mixed[:, LANES:]]
        for chip in range(chips):
            factor = jnp.exp(tops[chip] - top)
            total = total + factor * totals[chip]
            for k in range(2):
                part = parts[chip, k * LINES : (k + 1) * LINES].astype(jnp.float32)
                halves[k] = halves[k] + factor * part
        result = jnp.concatenate(halves, axis=1) / total
        heads = GROUP // 2
        for row in range(2):
            for s in range(STEPS):
                for a in range(heads):
                    at = row * QROWS + s * GROUP + a
                    low[row, s : s + 1, a * HD : (a + 1) * HD] = result[at : at + 1]
                    at = at + heads
                    high[row, s : s + 1, a * HD : (a + 1) * HD] = result[at : at + 1]


def combine(info, parts, query, fresh):
    heads = GROUP // 2
    shape = pltpu.VMEM((2, STEPS, heads * HD), jnp.float32)
    return pl.pallas_call(
        combine_kernel,
        name="combine_parts",
        out_shape=(shape, shape),
        in_specs=[SMEM, VMEM, VMEM, VMEM],
        out_specs=(VMEM, VMEM),
        compiler_params=PARAMS,
        cost_estimate=FREE,
    )(info, near(parts), near(query), near(fresh))


def delta_kernel(decay, beta, states, query, key, value, gate, out, final, rows):
    batch, steps, heads_k, width = key.shape
    heads_v = value.shape[2]
    ratio = heads_v // heads_k
    keys_at = batch * steps * heads_k

    def column(row, step, head):
        return (row * steps + step) * heads_k + head

    rows[...] = jnp.zeros_like(rows)
    for row in range(batch):
        for step in range(steps):
            at = column(row, step, 0)
            q = query[row, step].astype(jnp.float32)
            k = key[row, step].astype(jnp.float32)
            q = q * lax.rsqrt(jnp.sum(q * q, -1, keepdims=True) + 1e-06) * width ** (-0.5)
            k = k * lax.rsqrt(jnp.sum(k * k, -1, keepdims=True) + 1e-06)
            rows[at : at + heads_k] = q
            rows[keys_at + at : keys_at + at + heads_k] = k
    columns = jnp.transpose(rows[...])
    for row in range(batch):
        made = [[] for _ in range(steps)]
        values = [value[row, step].astype(jnp.float32) for step in range(steps)]
        for head in range(heads_v):
            state = states[row, head].astype(jnp.float32)
            for step in range(steps):
                at = column(row, step, head // ratio)
                q = columns[:, at : at + 1]
                k = columns[:, keys_at + at : keys_at + at + 1]
                rate = decay[row, step, head]
                recalled = jnp.sum(k * state, axis=0, keepdims=True)
                change = beta[row, step, head] * (values[step][head : head + 1] - rate * recalled)
                state = rate * state + k * change
                made[step].append(jnp.sum(q * state, axis=0, keepdims=True))
            final[row, head] = state
        for step in range(steps):
            read = jnp.concatenate(made[step], axis=0)
            read = read * lax.rsqrt(jnp.mean(read * read, -1, keepdims=True) + 1e-06)
            level = gate[row, step].astype(jnp.float32)
            out[row, step] = (read * (level * jax.nn.sigmoid(level))).astype(out.dtype)


def delta_rule(states, query, key, value, decay, beta, gate):
    width = key.shape[-1]
    return pl.pallas_call(
        delta_kernel,
        name="delta_rule",
        out_shape=(
            jax.ShapeDtypeStruct(value.shape, jnp.bfloat16),
            jax.ShapeDtypeStruct(states.shape, jnp.float32),
        ),
        in_specs=[SMEM, SMEM] + [VMEM] * 5,
        out_specs=(VMEM, VMEM),
        scratch_shapes=[pltpu.VMEM((width, width), jnp.float32)],
        compiler_params=PARAMS,
        cost_estimate=FREE,
    )(decay, beta, states, query, key, value, gate)


def on_device(
    kv_cache,
    lin_states,
    row_order,
    prompt_lengths,
    att_query,
    new_kv,
    att_gate,
    lin_query,
    lin_key,
    lin_value,
    lin_decay,
    lin_beta,
    lin_gate,
):
    wide_count = lax.axis_size("wide")
    chips = wide_count // 2
    head_index = lax.axis_index("head")
    place = jnp.stack([head_index, lax.axis_index("wide")]).astype(jnp.int32)
    info = jnp.concatenate([row_order, prompt_lengths, place])

    def across(array):
        pairs = [(i, i ^ 1) for i in range(wide_count)]
        return lax.ppermute(array, "wide", pairs)

    def after(array, *others):
        return lax.optimization_barrier((array, *others))[0]

    same_core = [[2 * k + c for k in range(chips)] for c in range(2)]

    def between_chips(array):
        return lax.all_to_all(array, "wide", 0, 0, tiled=True, axis_index_groups=same_core)

    mine = lax.dynamic_slice_in_dim(att_query, (head_index % KVH) * GROUP, GROUP, 2)
    copies = jnp.broadcast_to(mine.reshape(1, 2, QROWS, HD), (chips, 2, QROWS, HD))
    query = hold(between_chips(copies.reshape(2 * chips, QROWS, HD)), 30 * 10**9)

    taken = lin_states.at[row_order].get(mode="promise_in_bounds", unique_indices=True)
    taken = taken.astype(jnp.bfloat16)
    made = gather_rows(info, kv_cache, 0, CHUNK, 1)
    made += gather_rows(
        after(info, taken, *made), kv_cache, CHUNK, CHUNK * (CHUNKS - 1), CHUNKS - 1
    )
    swapped = [across(part) for part in made]

    weights = []
    for chunk in range(CHUNKS):
        held = after(info, *weights)
        weights.append(score_rows(held, query, kv_cache, swapped[chunk], chunk))
    moved = [lax.ppermute(made, "head", [(0, 2), (1, 3)]) for made in weights]

    states = lax.all_to_all(
        after(taken, weights[-1]), "wide", split_axis=0, concat_axis=2, tiled=True
    )

    payload, rows = None, None
    for chunk in range(CHUNKS):
        cost = 10 * 10**9 if chunk == CHUNKS - 1 else 100 * 10**6
        payload, rows = mix_rows(
            info, moved[chunk], kv_cache, swapped, chunk, payload, rows, cost
        )
    parts = between_chips(payload)
    lin_out, final_states = delta_rule(
        after(states, payload), lin_query, lin_key, lin_value, lin_decay, lin_beta, lin_gate
    )
    low, high = combine(info, parts, att_query, after(new_kv, lin_out))
    low_here = lax.ppermute(low, "head", [(2, 0), (3, 2)])
    high_here = lax.ppermute(high, "head", [(2, 1)])
    result = jnp.where(
        head_index == 3, high, jnp.where(head_index == 1, high_here, low_here)
    )
    att_out = (result * jax.nn.sigmoid(att_gate.astype(jnp.float32))).astype(jnp.bfloat16)

    return (att_out, lin_out, final_states)


def solution(mesh):
    placed = (
        P(None, "wide", "head"),
        P(None, "head", "wide", None),
        P(),
        P(),
        P("wide", None, None, None),
        P("wide", None, None),
        P("wide", None, "head"),
        P("wide", None, "head", None),
        P("wide", None, "head", None),
        P("wide", None, "head", None),
        P("wide", None, "head"),
        P("wide", None, "head"),
        P("wide", None, "head", None),
    )
    return jax.shard_map(
        on_device,
        mesh=mesh,
        in_specs=placed,
        out_specs=(
            P("wide", None, "head"),
            P("wide", None, "head", None),
            P("wide", "head", None, None),
        ),
        check_vma=False,
    )
```

```python
import functools

import jax
import jax.numpy as jnp
from jax import lax
from jax.experimental import pallas as pl
from jax.experimental.pallas import tpu as pltpu
from jax.sharding import PartitionSpec as P

HQ = 16
KVH = 2
HD = 256
STEPS = 3
GROUP = HQ // KVH
QROWS = STEPS * GROUP
LANES = 128
NEGATIVE = -1e30

SLOTS = 32
SIZES = (8, 12, 12)
FIRSTS = (0, 8, 20)
CHUNKS = 3
GROUPS = ((8,), (4, 8), (4, 8))
NT = (((1,), (1,)), ((), ()))
LIMIT = 16 * 2**20
VMEM = pl.BlockSpec(memory_space=pltpu.VMEM)
SMEM = pl.BlockSpec(memory_space=pltpu.SMEM)
ANY = pl.BlockSpec(memory_space=pltpu.HBM)
PARAMS = pltpu.CompilerParams(vmem_limit_bytes=LIMIT)
FREE = pl.CostEstimate(flops=0, bytes_accessed=0, transcendentals=0)

def near(array):
    return pltpu.with_memory_space_constraint(array, pltpu.VMEM)


def far(array):
    return pltpu.with_memory_space_constraint(array, pltpu.HBM)


def prefill_row(order, slot, other=0):
    core = (lax.axis_index("wide") & 1) ^ other
    return order[4 * (slot // 2) + 2 * core + slot % 2]


def gather_kernel(order, cache, *refs, chunks):
    outs, (held, arrived, left) = refs[:-3], refs[-3:]
    reads, writes = [], []
    for chunk, out in zip(chunks, outs):
        for n in range(SIZES[chunk]):
            at = len(reads)
            reads.append(
                pltpu.make_async_copy(
                    cache.at[prefill_row(order, FIRSTS[chunk] + n, 1)], held.at[at], arrived.at[at]
                )
            )
            writes.append(pltpu.make_async_copy(held.at[at], out.at[n], left.at[at]))
    for read in reads:
        read.start()
    for read, write in zip(reads, writes):
        read.wait()
        write.start()
    for write in writes:
        write.wait()


def gather_rows(order, cache, chunks):
    count = sum(SIZES[chunk] for chunk in chunks)
    copies = pltpu.SemaphoreType.DMA((count,))
    return pl.pallas_call(
        functools.partial(gather_kernel, chunks=chunks),
        name="gather_rows",
        out_shape=[pltpu.HBM((SIZES[c], *cache.shape[1:]), cache.dtype) for c in chunks],
        in_specs=[SMEM, ANY],
        out_specs=[ANY] * len(chunks),
        scratch_shapes=[held_rows(cache, count), copies, copies],
        compiler_params=PARAMS,
        cost_estimate=FREE,
    )(far(order), far(cache))


def hold_kernel(array, out):
    pass


def hold(array, cost):
    return pl.pallas_call(
        hold_kernel,
        name="hold",
        out_shape=pltpu.VMEM(array.shape, array.dtype),
        in_specs=[VMEM],
        out_specs=VMEM,
        input_output_aliases={0: 0},
        compiler_params=PARAMS,
        cost_estimate=pl.CostEstimate(flops=cost, bytes_accessed=0, transcendentals=0),
    )(near(array))


def fetches(order, cache, swapped, own, other, arrived, chunk):
    groups, first = {}, 0
    for at, size in enumerate(GROUPS[chunk]):
        span = pl.ds(first, size)
        copies = [
            pltpu.make_async_copy(
                swapped.at[span], other.at[span], arrived.at[SIZES[chunk] + at]
            )
        ] + [
            pltpu.make_async_copy(
                cache.at[prefill_row(order, FIRSTS[chunk] + n)], own.at[n], arrived.at[n]
            )
            for n in range(first, first + size)
        ]
        groups[first] = copies
        first += size
    return groups


def start(groups):
    for copies in groups.values():
        for copy in copies:
            copy.start()


def wait(groups, first):
    for copy in groups.get(first, ()):
        copy.wait()


def held_rows(cache, size):
    return pltpu.VMEM((size, *cache.shape[1:]), cache.dtype)


def arrivals(chunk):
    return pltpu.SemaphoreType.DMA((SIZES[chunk] + len(GROUPS[chunk]),))


def score_kernel(order, lengths, query, cache, swapped, out, own, other, arrived, *, chunk):
    size = SIZES[chunk]
    span = own.shape[1]
    width = 2 * span

    @pl.when(lax.axis_index("head") < 2)
    def _():
        groups = fetches(order, cache, swapped, own, other, arrived, chunk)
        start(groups)
        lane = lax.broadcasted_iota(jnp.int32, (QROWS, LANES), 1)
        column = lax.broadcasted_iota(jnp.int32, (QROWS, span), 1)
        wide = lax.axis_index("wide")
        position = jnp.concatenate([column + wide * span, column + (wide ^ 1) * span], axis=1)
        extra = jnp.zeros((QROWS, LANES), jnp.float32)
        for n in range(size):
            wait(groups, n)
            slot = FIRSTS[chunk] + n
            q = query[slot]
            scores = jnp.concatenate(
                [
                    lax.dot_general(q, own[n], NT, preferred_element_type=jnp.float32),
                    lax.dot_general(q, other[n], NT, preferred_element_type=jnp.float32),
                ],
                axis=1,
            ) * (HD ** (-0.5))
            valid = position < lengths[prefill_row(order, slot)]
            scores = jnp.where(valid, scores, NEGATIVE)
            top = jnp.max(scores, axis=1, keepdims=True)
            top = top.astype(jnp.bfloat16).astype(jnp.float32)
            weights = jnp.where(valid, jnp.exp(scores - top), 0.0)
            total = jnp.sum(weights, axis=1, keepdims=True)
            coarse = total.astype(jnp.bfloat16).astype(jnp.float32)
            out[:, n * width : (n + 1) * width] = weights.astype(out.dtype)
            extra = jnp.where(lane == n, top, extra)
            extra = jnp.where(lane == n + size, coarse, extra)
            extra = jnp.where(lane == n + 2 * size, total - coarse, extra)
        out[:, size * width :] = extra.astype(out.dtype)


def score_rows(order, lengths, query, cache, swapped, chunk):
    size = SIZES[chunk]
    rows = held_rows(cache, size)
    return pl.pallas_call(
        functools.partial(score_kernel, chunk=chunk),
        name="score_rows",
        out_shape=pltpu.VMEM((QROWS, size * 2 * cache.shape[1] + LANES), jnp.bfloat16),
        in_specs=[SMEM, SMEM, VMEM, ANY, ANY],
        out_specs=VMEM,
        scratch_shapes=[rows, rows, arrivals(chunk)],
        compiler_params=PARAMS,
        cost_estimate=FREE,
    )(far(order), far(lengths), near(query), far(cache), far(swapped))


LINES = 2 * QROWS
SLAB = 2 * LINES + 16
EXTRAS = 8


def mix_kernel(order, weights, *refs, chunk):
    last = chunk + 1 == CHUNKS
    fetch_last = chunk + 2 == CHUNKS
    made, left = refs[-2:]
    if last:
        own, other = refs[:2]
        out = refs[-3]
    elif fetch_last:
        cache, swapped, swapped_last = refs[:3]
        out, own_last, other_last, own, other, arrived, arrived_last = refs[-9:-2]
    else:
        cache, swapped = refs[:2]
        out, own, other, arrived = refs[-6:-2]
    size = SIZES[chunk]
    span = own.shape[1]
    width = 2 * span

    @pl.when(lax.axis_index("head") >= 2)
    def _():
        if not last:
            groups = fetches(order, cache, swapped, own, other, arrived, chunk)
            start(groups)
        if fetch_last:
            groups_last = fetches(
                order, cache, swapped_last, own_last, other_last, arrived_last, chunk + 1
            )
            start(groups_last)
        extra = weights[:, size * width :].astype(jnp.float32)
        extra = jnp.concatenate([extra, jnp.zeros((LANES - QROWS, LANES), jnp.float32)], axis=0)
        extra = jnp.transpose(extra)
        blank = jnp.zeros((16 - 6, LANES), jnp.float32)
        for pair in range(size // 2):
            if not last:
                wait(groups, 2 * pair)
            rows, lines = [], []
            for n in (2 * pair, 2 * pair + 1):
                at = n * width
                rows.append(
                    jnp.dot(
                        weights[:, at : at + span], own[n], preferred_element_type=jnp.float32
                    )
                    + jnp.dot(
                        weights[:, at + span : at + width],
                        other[n],
                        preferred_element_type=jnp.float32,
                    )
                )
                lines += [extra[n + k * size : n + k * size + 1] for k in range(3)]
            slab = [row[:, :LANES] for row in rows] + [row[:, LANES:] for row in rows]
            made[pair] = jnp.concatenate([*slab, *lines, blank], axis=0).astype(made.dtype)
        copy = pltpu.make_async_copy(
            made, out.at[pl.ds(FIRSTS[chunk] // 2, size // 2)], left.at[0]
        )
        copy.start()
        copy.wait()
        if fetch_last:
            for first in groups_last:
                wait(groups_last, first)


def mix_rows(order, weights, cache, swapped, chunk, before, rows, cost):
    last = chunk + 1 == CHUNKS
    fetch_last = chunk + 2 == CHUNKS
    size = SIZES[chunk]
    held, held_last = held_rows(cache, size), held_rows(cache, SIZES[-1])
    payload = pltpu.HBM((SLOTS // 2, SLAB, LANES), jnp.bfloat16)
    if last:
        in_specs = [SMEM, VMEM, VMEM, VMEM]
        operands = [far(order), near(weights), near(rows[0]), near(rows[1])]
    else:
        in_specs = [SMEM, VMEM, ANY, ANY]
        operands = [far(order), near(weights), far(cache), far(swapped[chunk])]
    if fetch_last:
        in_specs.append(ANY)
        operands.append(far(swapped[chunk + 1]))
    aliases = {}
    if before is not None:
        in_specs.append(ANY)
        aliases = {len(operands): 0}
        operands.append(far(before))
    made = pl.pallas_call(
        functools.partial(mix_kernel, chunk=chunk),
        name="mix_rows",
        out_shape=[payload] + ([held_last, held_last] if fetch_last else []),
        in_specs=in_specs,
        out_specs=[ANY] + ([VMEM, VMEM] if fetch_last else []),
        input_output_aliases=aliases,
        scratch_shapes=([] if last else [held, held, arrivals(chunk)])
        + ([arrivals(CHUNKS - 1)] if fetch_last else [])
        + [pltpu.VMEM((size // 2, SLAB, LANES), jnp.bfloat16), pltpu.SemaphoreType.DMA((1,))],
        compiler_params=PARAMS,
        cost_estimate=pl.CostEstimate(flops=cost, bytes_accessed=0, transcendentals=0),
    )(*operands)
    return made[0], made[1:]


def combine_kernel(parts, query, fresh, low, high):
    @pl.when(lax.axis_index("head") >= 2)
    def _():
        chips = parts.shape[0]
        second = lax.axis_index("head") & 1
        half = KVH * HD
        extras = jnp.stack(
            [parts[chip, 2 * LINES :].astype(jnp.float32)[:EXTRAS] for chip in range(chips)]
        )
        tops = [extras[:, 3 * row] for row in range(2)]
        totals = [extras[:, 3 * row + 1] + extras[:, 3 * row + 2] for row in range(2)]
        step = lax.broadcasted_iota(jnp.int32, (QROWS, STEPS), 0) // GROUP
        time = lax.broadcasted_iota(jnp.int32, (QROWS, STEPS), 1)
        keep = time <= step
        scores, values = [], []
        for row in range(2):
            news = fresh[row].astype(jnp.float32)
            keys = jnp.where(second == 1, news[:, HD:half], news[:, :HD])
            values.append(jnp.where(second == 1, news[:, half + HD :], news[:, half : half + HD]))
            q = jnp.where(second == 1, query[row, :, GROUP:], query[row, :, :GROUP])
            q = q.reshape(QROWS, HD).astype(jnp.float32)
            columns = [
                jnp.sum(q * keys[t : t + 1], axis=1, keepdims=True) for t in range(STEPS)
            ]
            score = jnp.concatenate(columns, axis=1) * (HD ** (-0.5))
            scores.append(jnp.where(keep, score, NEGATIVE))
        lines, marks = [], []
        for row in range(2):
            top = jnp.max(tops[row], axis=0, keepdims=True)
            factors = jnp.exp(tops[row] - top)
            lines += [top, jnp.sum(factors * totals[row], axis=0, keepdims=True)]
            marks.append(factors)
        blank = jnp.zeros((LANES - 4 - 2 * chips, LANES), jnp.float32)
        columns = jnp.transpose(jnp.concatenate([*marks, *lines, blank], axis=0))[:QROWS]
        halves = []
        for row in range(2):
            at = 2 * chips + 2 * row
            cached = columns[:, at : at + 1]
            top = jnp.maximum(cached, jnp.max(scores[row], axis=1, keepdims=True))
            scale = jnp.exp(cached - top)
            probs = jnp.where(keep, jnp.exp(scores[row] - top), 0.0)
            total = columns[:, at + 1 : at + 2] * scale + jnp.sum(probs, axis=1, keepdims=True)
            probs = probs.astype(jnp.bfloat16).astype(jnp.float32)
            mixed = sum(probs[:, t : t + 1] * values[row][t : t + 1] for t in range(STEPS))
            first = row * QROWS
            sides = []
            for k in range(2):
                acc = jnp.zeros((QROWS, LANES), jnp.float32)
                for chip in range(chips):
                    span = slice(k * LINES + first, k * LINES + first + QROWS)
                    part = parts[chip, span].astype(jnp.float32)
                    at = row * chips + chip
                    acc = acc + columns[:, at : at + 1] * part
                sides.append(acc * scale + mixed[:, k * LANES : (k + 1) * LANES])
            halves.append(jnp.concatenate(sides, axis=1) / total)
        heads = GROUP // 2
        for row in range(2):
            for s in range(STEPS):
                for a in range(heads):
                    at = s * GROUP + a
                    span = slice(a * HD, (a + 1) * HD)
                    low[s, row : row + 1, span] = halves[row][at : at + 1]
                    high[s, row : row + 1, span] = halves[row][at + heads : at + heads + 1]


def combine(parts, query, fresh):
    heads = GROUP // 2
    shape = pltpu.VMEM((STEPS, 2, heads * HD), jnp.float32)
    return pl.pallas_call(
        combine_kernel,
        name="combine_parts",
        out_shape=(shape, shape),
        in_specs=[VMEM, VMEM, VMEM],
        out_specs=(VMEM, VMEM),
        compiler_params=PARAMS,
        cost_estimate=FREE,
    )(near(parts), near(query), near(fresh))


NEAR = 4


def block_kernel(*refs, moves):
    for target, at, source, place in moves:
        refs[target][at] = refs[source][place].astype(refs[target].dtype)


def move_blocks(name, arrays, shapes, moves):
    count = len(arrays)
    return pl.pallas_call(
        functools.partial(
            block_kernel, moves=[(count + t, at, source, place) for t, at, source, place in moves]
        ),
        name=name,
        out_shape=[pltpu.VMEM(shape, jnp.bfloat16) for shape in shapes],
        in_specs=[VMEM] * count,
        out_specs=[VMEM] * len(shapes),
        compiler_params=PARAMS,
        cost_estimate=FREE,
    )(*[near(array) for array in arrays])


def split_kernel(order, states, mine, theirs):
    wide = lax.axis_index("wide")
    for z in range(NEAR):
        for y in range(NEAR):
            chip = (wide >> 1) ^ (4 * y + z)
            for row in range(2):
                at = 4 * chip + 2 * (wide & 1) + row
                mine[z, y, row] = states[order[at]].astype(mine.dtype)
                theirs[z, y, row] = states[order[at ^ 2]].astype(theirs.dtype)


def split_states(order, states):
    shape = pltpu.VMEM((NEAR, NEAR, 2, *states.shape[1:]), jnp.bfloat16)
    return pl.pallas_call(
        split_kernel,
        name="split_states",
        out_shape=(shape, shape),
        in_specs=[SMEM, VMEM],
        out_specs=(VMEM, VMEM),
        compiler_params=PARAMS,
        cost_estimate=FREE,
    )(far(order), near(states))


def along_z(mine, other):
    shape = (2, *mine.shape[1:])
    moves = [(z, core, core, z) for z in range(NEAR) for core in range(2)]
    return move_blocks("pack_z", [mine, other], [shape] * NEAR, moves)


def along_y(blocks):
    shape = (NEAR, 2, *blocks[0].shape[2:])
    moves = [
        (y, (z, core), z, (core, y)) for y in range(NEAR) for z in range(NEAR) for core in range(2)
    ]
    return move_blocks("pack_y", blocks, [shape] * NEAR, moves)


def join_kernel(*refs):
    blocks, out = refs[:NEAR], refs[NEAR]
    wide = lax.axis_index("wide")
    for y in range(NEAR):
        for z in range(NEAR):
            for core in range(2):
                out[wide ^ (8 * y + 2 * z + core)] = blocks[y][z, core]


def join_states(blocks):
    shape = (2 * NEAR * NEAR, *blocks[0].shape[2:])
    return pl.pallas_call(
        join_kernel,
        name="join_states",
        out_shape=pltpu.VMEM(shape, jnp.bfloat16),
        in_specs=[VMEM] * NEAR,
        out_specs=VMEM,
        compiler_params=PARAMS,
        cost_estimate=FREE,
    )(*[near(block) for block in blocks])


def delta_kernel(decay, beta, states, query, key, value, gate, out, final, rows):
    batch, steps, heads_k, width = key.shape
    heads_v = value.shape[2]
    ratio = heads_v // heads_k
    keys_at = batch * steps * heads_k

    def column(row, step, head):
        return (row * steps + step) * heads_k + head

    rows[...] = jnp.zeros_like(rows)
    for row in range(batch):
        for step in range(steps):
            at = column(row, step, 0)
            q = query[row, step].astype(jnp.float32)
            k = key[row, step].astype(jnp.float32)
            q = q * lax.rsqrt(jnp.sum(q * q, -1, keepdims=True) + 1e-06) * width ** (-0.5)
            k = k * lax.rsqrt(jnp.sum(k * k, -1, keepdims=True) + 1e-06)
            rows[at : at + heads_k] = q
            rows[keys_at + at : keys_at + at + heads_k] = k
    columns = jnp.transpose(rows[...])
    for row in range(batch):
        made = [[] for _ in range(steps)]
        values = [value[row, step].astype(jnp.float32) for step in range(steps)]
        for head in range(heads_v):
            state = states[row, head].astype(jnp.float32)
            for step in range(steps):
                at = column(row, step, head // ratio)
                q = columns[:, at : at + 1]
                k = columns[:, keys_at + at : keys_at + at + 1]
                rate = decay[row, step, head]
                recalled = jnp.sum(k * state, axis=0, keepdims=True)
                change = beta[row, step, head] * (values[step][head : head + 1] - rate * recalled)
                state = rate * state + k * change
                made[step].append(jnp.sum(q * state, axis=0, keepdims=True))
            final[row, head] = state
        for step in range(steps):
            read = jnp.concatenate(made[step], axis=0)
            read = read * lax.rsqrt(jnp.mean(read * read, -1, keepdims=True) + 1e-06)
            level = gate[row, step].astype(jnp.float32)
            out[row, step] = (read * (level * jax.nn.sigmoid(level))).astype(out.dtype)


def delta_rule(states, query, key, value, decay, beta, gate):
    width = key.shape[-1]
    return pl.pallas_call(
        delta_kernel,
        name="delta_rule",
        out_shape=(
            jax.ShapeDtypeStruct(value.shape, jnp.bfloat16),
            jax.ShapeDtypeStruct(states.shape, jnp.float32),
        ),
        in_specs=[SMEM, SMEM] + [VMEM] * 5,
        out_specs=(VMEM, VMEM),
        scratch_shapes=[pltpu.VMEM((width, width), jnp.float32)],
        compiler_params=PARAMS,
        cost_estimate=FREE,
    )(decay, beta, states, query, key, value, gate)


def on_device(
    kv_cache,
    lin_states,
    row_order,
    prompt_lengths,
    att_query,
    new_kv,
    att_gate,
    lin_query,
    lin_key,
    lin_value,
    lin_decay,
    lin_beta,
    lin_gate,
):
    wide_count = lax.axis_size("wide")
    chips = wide_count // 2
    head_index = lax.axis_index("head")
    def across(array, distance=1):
        pairs = [(i, i ^ distance) for i in range(wide_count)]
        return lax.ppermute(array, "wide", pairs)

    def after(array, *others):
        return lax.optimization_barrier((array, *others))[0]

    same_core = [[2 * k + c for k in range(chips)] for c in range(2)]

    def between_chips(array):
        return lax.all_to_all(array, "wide", 0, 0, tiled=True, axis_index_groups=same_core)

    sides = [
        jnp.broadcast_to(side.reshape(1, 2, QROWS, HD), (chips, 2, QROWS, HD))
        for side in (att_query[:, :, :GROUP], att_query[:, :, GROUP:])
    ]
    copies = jnp.where(head_index % KVH == 1, sides[1], sides[0])
    query = hold(between_chips(copies.reshape(2 * chips, QROWS, HD)), 30 * 10**9)

    made = gather_rows(row_order, kv_cache, (0,))
    made += gather_rows(after(row_order, *made), kv_cache, tuple(range(1, CHUNKS)))
    rows_all, heads, depth, width = lin_states.shape
    mine, theirs = split_states(
        after(row_order, *made), lin_states.reshape(rows_all, heads * depth, width)
    )
    swapped = [across(part) for part in made]
    other = across(theirs)

    weights = []
    for chunk in range(CHUNKS):
        order = after(row_order, theirs, *weights)
        weights.append(
            score_rows(order, prompt_lengths, query, kv_cache, swapped[chunk], chunk)
        )
    moved = [lax.ppermute(made, "head", [(0, 2), (1, 3)]) for made in weights]

    blocks = along_z(after(mine, weights[-1]), other)
    blocks = [blocks[0]] + [across(block, 2 * z) for z, block in enumerate(blocks[1:], 1)]
    blocks = along_y(blocks)

    payload, rows = None, None
    for chunk in range(CHUNKS):
        cost = 10 * 10**9 if chunk + 1 == CHUNKS else 10**8
        payload, rows = mix_rows(
            after(row_order, weights[-1]), moved[chunk], kv_cache, swapped, chunk, payload, rows,
            cost,
        )
    parts = between_chips(after(payload, *blocks))
    blocks = [blocks[0]] + [across(block, 8 * y) for y, block in enumerate(blocks[1:], 1)]
    states = join_states(blocks).reshape(wide_count, 2, heads, depth, width)
    states = states.transpose(1, 2, 0, 3, 4).reshape(2, heads, wide_count * depth, width)
    lin_out, final_states = delta_rule(
        states, lin_query, lin_key, lin_value, lin_decay, lin_beta, lin_gate
    )
    low, high = combine(parts, att_query, after(new_kv, lin_out))
    low_here = lax.ppermute(low, "head", [(2, 0), (3, 2)])
    high_here = lax.ppermute(high, "head", [(2, 1)])
    result = jnp.where(
        head_index == 3, high, jnp.where(head_index == 1, high_here, low_here)
    )
    gate = jnp.transpose(att_gate, (1, 0, 2)).astype(jnp.float32)
    att_out = (result * jax.nn.sigmoid(gate)).astype(jnp.bfloat16)
    att_out = jnp.transpose(att_out, (1, 0, 2))
    return (att_out, lin_out, final_states)


def solution(mesh):
    placed = (
        P(None, "wide", "head"),
        P(None, "head", "wide", None),
        P(),
        P(),
        P("wide", None, None, None),
        P("wide", None, None),
        P("wide", None, "head"),
        P("wide", None, "head", None),
        P("wide", None, "head", None),
        P("wide", None, "head", None),
        P("wide", None, "head"),
        P("wide", None, "head"),
        P("wide", None, "head", None),
    )
    return jax.shard_map(
        on_device,
        mesh=mesh,
        in_specs=placed,
        out_specs=(
            P("wide", None, "head"),
            P("wide", None, "head", None),
            P("wide", "head", None, None),
        ),
        check_vma=False,
    )
```

```python
import functools

import jax
import jax.numpy as jnp
from jax import lax
from jax.experimental import pallas as pl
from jax.experimental.pallas import tpu as pltpu
from jax.sharding import PartitionSpec as P

HQ = 16
KVH = 2
HD = 256
STEPS = 3
GROUP = HQ // KVH
QROWS = STEPS * GROUP
LANES = 128
NEGATIVE = -1e30

SLOTS = 32
SIZES = (8, 12, 12)
FIRSTS = (0, 8, 20)
CHUNKS = 3
GROUPS = ((8,), (4, 8), (4, 8))
NT = (((1,), (1,)), ((), ()))
LIMIT = 16 * 2**20
VMEM = pl.BlockSpec(memory_space=pltpu.VMEM)
SMEM = pl.BlockSpec(memory_space=pltpu.SMEM)
ANY = pl.BlockSpec(memory_space=pltpu.HBM)
PARAMS = pltpu.CompilerParams(vmem_limit_bytes=LIMIT)
FREE = pl.CostEstimate(flops=0, bytes_accessed=0, transcendentals=0)

def near(array):
    return pltpu.with_memory_space_constraint(array, pltpu.VMEM)


def far(array):
    return pltpu.with_memory_space_constraint(array, pltpu.HBM)


def prefill_row(order, slot, other=0):
    core = (lax.axis_index("wide") & 1) ^ other
    return order[4 * (slot // 2) + 2 * core + slot % 2]


def gather_kernel(order, cache, out, held, arrived, left, *, first):
    count = out.shape[0]
    reads = [
        pltpu.make_async_copy(cache.at[prefill_row(order, first + n, 1)], held.at[n], arrived.at[n])
        for n in range(count)
    ]
    writes = [pltpu.make_async_copy(held.at[n], out.at[n], left.at[n]) for n in range(count)]
    for read in reads:
        read.start()
    for read, write in zip(reads, writes):
        read.wait()
        write.start()
    for write in writes:
        write.wait()


def gather_rows(order, cache, first, count):
    copies = pltpu.SemaphoreType.DMA((count,))
    return pl.pallas_call(
        functools.partial(gather_kernel, first=first),
        name="gather_rows",
        out_shape=pltpu.HBM((count, *cache.shape[1:]), cache.dtype),
        in_specs=[SMEM, ANY],
        out_specs=ANY,
        scratch_shapes=[held_rows(cache, count), copies, copies],
        compiler_params=PARAMS,
        cost_estimate=FREE,
    )(far(order), far(cache))


def hold_kernel(*refs):
    pass


def hold(arrays, cost):
    count = len(arrays)
    return pl.pallas_call(
        hold_kernel,
        name="hold",
        out_shape=[pltpu.VMEM(array.shape, array.dtype) for array in arrays],
        in_specs=[VMEM] * count,
        out_specs=[VMEM] * count,
        input_output_aliases={n: n for n in range(count)},
        compiler_params=PARAMS,
        cost_estimate=pl.CostEstimate(flops=cost, bytes_accessed=0, transcendentals=0),
    )(*[near(array) for array in arrays])


def fetches(order, cache, swapped, own, other, arrived, chunk):
    groups, first = {}, 0
    base = FIRSTS[chunk] - FIRSTS[1]
    for at, size in enumerate(GROUPS[chunk]):
        copies = [
            pltpu.make_async_copy(
                cache.at[prefill_row(order, FIRSTS[chunk] + n)], own.at[n], arrived.at[n]
            )
            for n in range(first, first + size)
        ]
        if chunk:
            copies.insert(
                0,
                pltpu.make_async_copy(
                    swapped.at[pl.ds(base + first, size)],
                    other.at[pl.ds(first, size)],
                    arrived.at[SIZES[chunk] + at],
                ),
            )
        groups[first] = copies
        first += size
    return groups


def start(groups):
    for copies in groups.values():
        for copy in copies:
            copy.start()


def wait(groups, first):
    for copy in groups.get(first, ()):
        copy.wait()


def held_rows(cache, size):
    return pltpu.VMEM((size, *cache.shape[1:]), cache.dtype)


def arrivals(chunk):
    return pltpu.SemaphoreType.DMA((SIZES[chunk] + len(GROUPS[chunk]),))


def score_kernel(order, lengths, query, cache, swapped, out, own, other, arrived, *, chunk):
    if not chunk:
        other = swapped
    size = SIZES[chunk]
    span = own.shape[1]
    width = 2 * span

    @pl.when(lax.axis_index("head") < 2)
    def _():
        groups = fetches(order, cache, swapped, own, other, arrived, chunk)
        start(groups)
        lane = lax.broadcasted_iota(jnp.int32, (QROWS, LANES), 1)
        column = lax.broadcasted_iota(jnp.int32, (QROWS, span), 1)
        wide = lax.axis_index("wide")
        position = jnp.concatenate([column + wide * span, column + (wide ^ 1) * span], axis=1)
        extra = jnp.zeros((QROWS, LANES), jnp.float32)
        for n in range(size):
            wait(groups, n)
            slot = FIRSTS[chunk] + n
            q = query[slot]
            scores = jnp.concatenate(
                [
                    lax.dot_general(q, own[n], NT, preferred_element_type=jnp.float32),
                    lax.dot_general(q, other[n], NT, preferred_element_type=jnp.float32),
                ],
                axis=1,
            ) * (HD ** (-0.5))
            valid = position < lengths[prefill_row(order, slot)]
            scores = jnp.where(valid, scores, NEGATIVE)
            top = jnp.max(scores, axis=1, keepdims=True)
            top = top.astype(jnp.bfloat16).astype(jnp.float32)
            weights = jnp.where(valid, jnp.exp(scores - top), 0.0)
            total = jnp.sum(weights, axis=1, keepdims=True)
            coarse = total.astype(jnp.bfloat16).astype(jnp.float32)
            out[:, n * width : (n + 1) * width] = weights.astype(out.dtype)
            extra = jnp.where(lane == n, top, extra)
            extra = jnp.where(lane == n + size, coarse, extra)
            extra = jnp.where(lane == n + 2 * size, total - coarse, extra)
        out[:, size * width :] = extra.astype(out.dtype)


def score_rows(order, lengths, query, cache, swapped, chunk):
    size = SIZES[chunk]
    rows = held_rows(cache, size)
    return pl.pallas_call(
        functools.partial(score_kernel, chunk=chunk),
        name="score_rows",
        out_shape=pltpu.VMEM((QROWS, size * 2 * cache.shape[1] + LANES), jnp.bfloat16),
        in_specs=[SMEM, SMEM, VMEM, ANY, ANY if chunk else VMEM],
        out_specs=VMEM,
        scratch_shapes=[rows, rows, arrivals(chunk)],
        compiler_params=PARAMS,
        cost_estimate=FREE,
    )(far(order), far(lengths), near(query), far(cache), (far if chunk else near)(swapped))


LINES = 2 * QROWS
SLAB = 2 * LINES + 16
EXTRAS = 8


def mix_kernel(order, weights, *refs, chunk):
    last = chunk + 1 == CHUNKS
    fetch_last = chunk + 2 == CHUNKS
    made, left = refs[-2:]
    if last:
        own, other = refs[:2]
        out = refs[-3]
    elif fetch_last:
        cache, swapped, swapped_last = refs[:3]
        out, own_last, other_last, own, other, arrived, arrived_last = refs[-9:-2]
    else:
        cache, other = refs[:2]
        swapped = None
        out, own, _, arrived = refs[-6:-2]
    size = SIZES[chunk]
    span = own.shape[1]
    width = 2 * span

    @pl.when(lax.axis_index("head") >= 2)
    def _():
        if not last:
            groups = fetches(order, cache, swapped, own, other, arrived, chunk)
            start(groups)
        if fetch_last:
            groups_last = fetches(
                order, cache, swapped_last, own_last, other_last, arrived_last, chunk + 1
            )
            start(groups_last)
        extra = weights[:, size * width :].astype(jnp.float32)
        extra = jnp.concatenate([extra, jnp.zeros((LANES - QROWS, LANES), jnp.float32)], axis=0)
        extra = jnp.transpose(extra)
        blank = jnp.zeros((16 - 6, LANES), jnp.float32)
        for pair in range(size // 2):
            if not last:
                wait(groups, 2 * pair)
            rows, lines = [], []
            for n in (2 * pair, 2 * pair + 1):
                at = n * width
                rows.append(
                    jnp.dot(
                        weights[:, at : at + span], own[n], preferred_element_type=jnp.float32
                    )
                    + jnp.dot(
                        weights[:, at + span : at + width],
                        other[n],
                        preferred_element_type=jnp.float32,
                    )
                )
                lines += [extra[n + k * size : n + k * size + 1] for k in range(3)]
            slab = [row[:, :LANES] for row in rows] + [row[:, LANES:] for row in rows]
            made[pair] = jnp.concatenate([*slab, *lines, blank], axis=0).astype(made.dtype)
        copy = pltpu.make_async_copy(
            made, out.at[pl.ds(FIRSTS[chunk] // 2, size // 2)], left.at[0]
        )
        copy.start()
        copy.wait()
        if fetch_last:
            for first in groups_last:
                wait(groups_last, first)


def mix_rows(order, weights, cache, swapped, chunk, before, rows, cost):
    last = chunk + 1 == CHUNKS
    fetch_last = chunk + 2 == CHUNKS
    size = SIZES[chunk]
    held, held_last = held_rows(cache, size), held_rows(cache, SIZES[-1])
    payload = pltpu.HBM((SLOTS // 2, SLAB, LANES), jnp.bfloat16)
    if last:
        in_specs = [SMEM, VMEM, VMEM, VMEM]
        operands = [far(order), near(weights), near(rows[0]), near(rows[1])]
    else:
        in_specs = [SMEM, VMEM, ANY, ANY if chunk else VMEM]
        operands = [
            far(order), near(weights), far(cache), (far if chunk else near)(swapped[chunk])
        ]
    if fetch_last:
        in_specs.append(ANY)
        operands.append(far(swapped[chunk + 1]))
    aliases = {}
    if before is not None:
        in_specs.append(ANY)
        aliases = {len(operands): 0}
        operands.append(far(before))
    made = pl.pallas_call(
        functools.partial(mix_kernel, chunk=chunk),
        name="mix_rows",
        out_shape=[payload] + ([held_last, held_last] if fetch_last else []),
        in_specs=in_specs,
        out_specs=[ANY] + ([VMEM, VMEM] if fetch_last else []),
        input_output_aliases=aliases,
        scratch_shapes=([] if last else [held, held, arrivals(chunk)])
        + ([arrivals(CHUNKS - 1)] if fetch_last else [])
        + [pltpu.VMEM((size // 2, SLAB, LANES), jnp.bfloat16), pltpu.SemaphoreType.DMA((1,))],
        compiler_params=PARAMS,
        cost_estimate=pl.CostEstimate(flops=cost, bytes_accessed=0, transcendentals=0),
    )(*operands)
    return made[0], made[1:]


def combine_kernel(parts, query, fresh, low, high):
    @pl.when(lax.axis_index("head") >= 2)
    def _():
        chips = parts.shape[0]
        second = lax.axis_index("head") & 1
        half = KVH * HD
        extras = jnp.stack(
            [parts[chip, 2 * LINES :].astype(jnp.float32)[:EXTRAS] for chip in range(chips)]
        )
        tops = [extras[:, 3 * row] for row in range(2)]
        totals = [extras[:, 3 * row + 1] + extras[:, 3 * row + 2] for row in range(2)]
        step = lax.broadcasted_iota(jnp.int32, (QROWS, STEPS), 0) // GROUP
        time = lax.broadcasted_iota(jnp.int32, (QROWS, STEPS), 1)
        keep = time <= step
        scores, values = [], []
        for row in range(2):
            news = fresh[row].astype(jnp.float32)
            keys = jnp.where(second == 1, news[:, HD:half], news[:, :HD])
            values.append(jnp.where(second == 1, news[:, half + HD :], news[:, half : half + HD]))
            q = jnp.where(second == 1, query[row, :, GROUP:], query[row, :, :GROUP])
            q = q.reshape(QROWS, HD).astype(jnp.float32)
            columns = [
                jnp.sum(q * keys[t : t + 1], axis=1, keepdims=True) for t in range(STEPS)
            ]
            score = jnp.concatenate(columns, axis=1) * (HD ** (-0.5))
            scores.append(jnp.where(keep, score, NEGATIVE))
        lines, marks = [], []
        for row in range(2):
            top = jnp.max(tops[row], axis=0, keepdims=True)
            factors = jnp.exp(tops[row] - top)
            lines += [top, jnp.sum(factors * totals[row], axis=0, keepdims=True)]
            marks.append(factors)
        blank = jnp.zeros((LANES - 4 - 2 * chips, LANES), jnp.float32)
        columns = jnp.transpose(jnp.concatenate([*marks, *lines, blank], axis=0))[:QROWS]
        halves = []
        for row in range(2):
            at = 2 * chips + 2 * row
            cached = columns[:, at : at + 1]
            top = jnp.maximum(cached, jnp.max(scores[row], axis=1, keepdims=True))
            scale = jnp.exp(cached - top)
            probs = jnp.where(keep, jnp.exp(scores[row] - top), 0.0)
            total = columns[:, at + 1 : at + 2] * scale + jnp.sum(probs, axis=1, keepdims=True)
            probs = probs.astype(jnp.bfloat16).astype(jnp.float32)
            mixed = sum(probs[:, t : t + 1] * values[row][t : t + 1] for t in range(STEPS))
            first = row * QROWS
            sides = []
            for k in range(2):
                acc = jnp.zeros((QROWS, LANES), jnp.float32)
                for chip in range(chips):
                    span = slice(k * LINES + first, k * LINES + first + QROWS)
                    part = parts[chip, span].astype(jnp.float32)
                    at = row * chips + chip
                    acc = acc + columns[:, at : at + 1] * part
                sides.append(acc * scale + mixed[:, k * LANES : (k + 1) * LANES])
            halves.append(jnp.concatenate(sides, axis=1) / total)
        heads = GROUP // 2
        for row in range(2):
            for s in range(STEPS):
                for a in range(heads):
                    at = s * GROUP + a
                    span = slice(a * HD, (a + 1) * HD)
                    low[s, row : row + 1, span] = halves[row][at : at + 1]
                    high[s, row : row + 1, span] = halves[row][at + heads : at + heads + 1]


def combine(parts, query, fresh):
    heads = GROUP // 2
    shape = pltpu.VMEM((STEPS, 2, heads * HD), jnp.float32)
    return pl.pallas_call(
        combine_kernel,
        name="combine_parts",
        out_shape=(shape, shape),
        in_specs=[VMEM, VMEM, VMEM],
        out_specs=(VMEM, VMEM),
        compiler_params=PARAMS,
        cost_estimate=FREE,
    )(near(parts), near(query), near(fresh))


NEAR = 4


def block_kernel(*refs, moves):
    for target, at, source, place in moves:
        refs[target][at] = refs[source][place].astype(refs[target].dtype)


def move_blocks(name, arrays, shapes, moves):
    count = len(arrays)
    return pl.pallas_call(
        functools.partial(
            block_kernel, moves=[(count + t, at, source, place) for t, at, source, place in moves]
        ),
        name=name,
        out_shape=[pltpu.VMEM(shape, jnp.bfloat16) for shape in shapes],
        in_specs=[VMEM] * count,
        out_specs=[VMEM] * len(shapes),
        compiler_params=PARAMS,
        cost_estimate=FREE,
    )(*[near(array) for array in arrays])


def split_kernel(order, states, mine, theirs):
    wide = lax.axis_index("wide")
    for z in range(NEAR):
        for y in range(NEAR):
            chip = (wide >> 1) ^ (4 * y + z)
            for row in range(2):
                at = 4 * chip + 2 * (wide & 1) + row
                mine[z, y, row] = states[order[at]].astype(mine.dtype)
                theirs[z, y, row] = states[order[at ^ 2]].astype(theirs.dtype)


def split_states(order, states):
    shape = pltpu.VMEM((NEAR, NEAR, 2, *states.shape[1:]), jnp.bfloat16)
    return pl.pallas_call(
        split_kernel,
        name="split_states",
        out_shape=(shape, shape),
        in_specs=[SMEM, VMEM],
        out_specs=(VMEM, VMEM),
        compiler_params=PARAMS,
        cost_estimate=FREE,
    )(far(order), near(states))


def along_z(mine, other):
    shape = (2, *mine.shape[1:])
    moves = [(z, core, core, z) for z in range(NEAR) for core in range(2)]
    return move_blocks("pack_z", [mine, other], [shape] * NEAR, moves)


def along_y(blocks):
    shape = (NEAR, 2, *blocks[0].shape[2:])
    moves = [
        (y, (z, core), z, (core, y)) for y in range(NEAR) for z in range(NEAR) for core in range(2)
    ]
    return move_blocks("pack_y", blocks, [shape] * NEAR, moves)


def join_kernel(*refs):
    blocks, out = refs[:NEAR], refs[NEAR]
    wide = lax.axis_index("wide")
    for y in range(NEAR):
        for z in range(NEAR):
            for core in range(2):
                out[wide ^ (8 * y + 2 * z + core)] = blocks[y][z, core]


def join_states(blocks):
    shape = (2 * NEAR * NEAR, *blocks[0].shape[2:])
    return pl.pallas_call(
        join_kernel,
        name="join_states",
        out_shape=pltpu.VMEM(shape, jnp.bfloat16),
        in_specs=[VMEM] * NEAR,
        out_specs=VMEM,
        compiler_params=PARAMS,
        cost_estimate=FREE,
    )(*[near(block) for block in blocks])


def delta_kernel(decay, beta, states, query, key, value, gate, out, final, rows):
    batch, steps, heads_k, width = key.shape
    heads_v = value.shape[2]
    ratio = heads_v // heads_k
    keys_at = batch * steps * heads_k

    def column(row, step, head):
        return (row * steps + step) * heads_k + head

    rows[...] = jnp.zeros_like(rows)
    for row in range(batch):
        for step in range(steps):
            at = column(row, step, 0)
            q = query[row, step].astype(jnp.float32)
            k = key[row, step].astype(jnp.float32)
            q = q * lax.rsqrt(jnp.sum(q * q, -1, keepdims=True) + 1e-06) * width ** (-0.5)
            k = k * lax.rsqrt(jnp.sum(k * k, -1, keepdims=True) + 1e-06)
            rows[at : at + heads_k] = q
            rows[keys_at + at : keys_at + at + heads_k] = k
    columns = jnp.transpose(rows[...])
    shape = (width, value.shape[3])
    for row in range(batch):
        made = [[] for _ in range(steps)]
        values = [value[row, step].astype(jnp.float32) for step in range(steps)]
        for head in range(heads_k):
            both = range(head * ratio, (head + 1) * ratio)
            held = [states[row, one].astype(jnp.float32) for one in both]
            for step in range(steps):
                at = column(row, step, head)
                q = jnp.broadcast_to(columns[:, at : at + 1], shape)
                k = jnp.broadcast_to(columns[:, keys_at + at : keys_at + at + 1], shape)
                for n, one in enumerate(both):
                    rate = decay[row, step, one]
                    recalled = jnp.sum(k * held[n], axis=0, keepdims=True)
                    change = beta[row, step, one] * (
                        values[step][one : one + 1] - rate * recalled
                    )
                    held[n] = rate * held[n] + k * change
                    made[step].append(jnp.sum(q * held[n], axis=0, keepdims=True))
            for n, one in enumerate(both):
                final[row, one] = held[n]
        for step in range(steps):
            read = jnp.concatenate(made[step], axis=0)
            read = read * lax.rsqrt(jnp.mean(read * read, -1, keepdims=True) + 1e-06)
            level = gate[row, step].astype(jnp.float32)
            out[row, step] = (read * (level * jax.nn.sigmoid(level))).astype(out.dtype)


def delta_rule(states, query, key, value, decay, beta, gate):
    width = key.shape[-1]
    return pl.pallas_call(
        delta_kernel,
        name="delta_rule",
        out_shape=(
            jax.ShapeDtypeStruct(value.shape, jnp.bfloat16),
            jax.ShapeDtypeStruct(states.shape, jnp.float32),
        ),
        in_specs=[SMEM, SMEM] + [VMEM] * 5,
        out_specs=(VMEM, VMEM),
        scratch_shapes=[pltpu.VMEM((width, width), jnp.float32)],
        compiler_params=PARAMS,
        cost_estimate=FREE,
    )(decay, beta, states, query, key, value, gate)


def on_device(
    kv_cache,
    lin_states,
    row_order,
    prompt_lengths,
    att_query,
    new_kv,
    att_gate,
    lin_query,
    lin_key,
    lin_value,
    lin_decay,
    lin_beta,
    lin_gate,
):
    wide_count = lax.axis_size("wide")
    chips = wide_count // 2
    head_index = lax.axis_index("head")
    def across(array, distance=1):
        pairs = [(i, i ^ distance) for i in range(wide_count)]
        return lax.ppermute(array, "wide", pairs)

    def after(array, *others):
        return lax.optimization_barrier((array, *others))[0]

    same_core = [[2 * k + c for k in range(chips)] for c in range(2)]

    def between_chips(array):
        return lax.all_to_all(array, "wide", 0, 0, tiled=True, axis_index_groups=same_core)

    sides = [
        jnp.broadcast_to(side.reshape(1, 2, QROWS, HD), (chips, 2, QROWS, HD))
        for side in (att_query[:, :, :GROUP], att_query[:, :, GROUP:])
    ]
    copies = jnp.where(head_index % KVH == 1, sides[1], sides[0])
    (query,) = hold([between_chips(copies.reshape(2 * chips, QROWS, HD))], 30 * 10**9)

    first = gather_rows(row_order, kv_cache, 0, FIRSTS[1])
    made = [first, gather_rows(after(row_order, first), kv_cache, FIRSTS[1], SLOTS - FIRSTS[1])]
    rows_all, heads, depth, width = lin_states.shape
    mine, theirs = split_states(
        after(row_order, *made), lin_states.reshape(rows_all, heads * depth, width)
    )
    query, first = hold([query, across(made[0])], 30 * 10**9)
    swapped = [first] + [across(made[1])] * (CHUNKS - 1)
    (other,) = hold([across(theirs)], 30 * 10**9)

    weights = []
    for chunk in range(CHUNKS):
        order = after(row_order, theirs, *weights)
        weights.append(
            score_rows(order, prompt_lengths, query, kv_cache, swapped[chunk], chunk)
        )
    moved = [lax.ppermute(made, "head", [(0, 2), (1, 3)]) for made in weights]

    blocks = along_z(after(mine, weights[-1]), other)
    crossed = [across(block, 2 * z) for z, block in enumerate(blocks[1:], 1)]
    blocks = [blocks[0], *hold(crossed, 10 * 10**9)]
    payload, rows = None, None
    for chunk in range(CHUNKS):
        cost = 10 * 10**9 if chunk + 1 == CHUNKS else 3 * 10**9
        payload, rows = mix_rows(
            after(row_order, weights[-1]), moved[chunk], kv_cache, swapped, chunk, payload, rows,
            cost,
        )
    parts = between_chips(payload)
    blocks = along_y([after(blocks[0], payload), *blocks[1:]])
    blocks = [blocks[0]] + [across(block, 8 * y) for y, block in enumerate(blocks[1:], 1)]
    low, high = combine(parts, att_query, new_kv)
    states = join_states([after(blocks[0], low), *blocks[1:]])
    states = states.reshape(wide_count, 2, heads, depth, width)
    states = states.transpose(1, 2, 0, 3, 4).reshape(2, heads, wide_count * depth, width)
    lin_out, final_states = delta_rule(
        states, lin_query, lin_key, lin_value, lin_decay, lin_beta, lin_gate
    )
    low_here = lax.ppermute(low, "head", [(2, 0), (3, 2)])
    high_here = lax.ppermute(high, "head", [(2, 1)])
    result = jnp.where(
        head_index == 3, high, jnp.where(head_index == 1, high_here, low_here)
    )
    gate = jnp.transpose(att_gate, (1, 0, 2)).astype(jnp.float32)
    att_out = (result * jax.nn.sigmoid(gate)).astype(jnp.bfloat16)
    att_out = jnp.transpose(att_out, (1, 0, 2))
    return (att_out, lin_out, final_states)


def solution(mesh):
    placed = (
        P(None, "wide", "head"),
        P(None, "head", "wide", None),
        P(),
        P(),
        P("wide", None, None, None),
        P("wide", None, None),
        P("wide", None, "head"),
        P("wide", None, "head", None),
        P("wide", None, "head", None),
        P("wide", None, "head", None),
        P("wide", None, "head"),
        P("wide", None, "head"),
        P("wide", None, "head", None),
    )
    return jax.shard_map(
        on_device,
        mesh=mesh,
        in_specs=placed,
        out_specs=(
            P("wide", None, "head"),
            P("wide", None, "head", None),
            P("wide", "head", None, None),
        ),
        check_vma=False,
    )
```

```python
import functools

import jax
import jax.numpy as jnp
from jax import lax
from jax.experimental import pallas as pl
from jax.experimental.pallas import tpu as pltpu
from jax.sharding import PartitionSpec as P

HQ = 16
KVH = 2
HD = 256
STEPS = 3
GROUP = HQ // KVH
QROWS = STEPS * GROUP
LANES = 128
NEGATIVE = -1e30

SLOTS = 32
SIZES = (12, 12, 8)
FIRSTS = (0, 12, 24)
CHUNKS = 3
GROUPS = ((4, 8), (4, 8), (8,))
NT = (((1,), (1,)), ((), ()))
LIMIT = 16 * 2**20
VMEM = pl.BlockSpec(memory_space=pltpu.VMEM)
SMEM = pl.BlockSpec(memory_space=pltpu.SMEM)
ANY = pl.BlockSpec(memory_space=pltpu.HBM)
PARAMS = pltpu.CompilerParams(vmem_limit_bytes=LIMIT)
FREE = pl.CostEstimate(flops=0, bytes_accessed=0, transcendentals=0)

def near(array):
    return pltpu.with_memory_space_constraint(array, pltpu.VMEM)


def far(array):
    return pltpu.with_memory_space_constraint(array, pltpu.HBM)


def prefill_row(order, slot, other=0):
    core = (lax.axis_index("wide") & 1) ^ other
    return order[4 * (slot // 2) + 2 * core + slot % 2]


def gather_kernel(order, cache, out, held, arrived, left, *, first):
    count = out.shape[0]
    reads = [
        pltpu.make_async_copy(cache.at[prefill_row(order, first + n, 1)], held.at[n], arrived.at[n])
        for n in range(count)
    ]
    writes = [pltpu.make_async_copy(held.at[n], out.at[n], left.at[n]) for n in range(count)]
    for read in reads:
        read.start()
    for read, write in zip(reads, writes):
        read.wait()
        write.start()
    for write in writes:
        write.wait()


def gather_rows(order, cache, first, count):
    copies = pltpu.SemaphoreType.DMA((count,))
    return pl.pallas_call(
        functools.partial(gather_kernel, first=first),
        name="gather_rows",
        out_shape=pltpu.HBM((count, *cache.shape[1:]), cache.dtype),
        in_specs=[SMEM, ANY],
        out_specs=ANY,
        scratch_shapes=[held_rows(cache, count), copies, copies],
        compiler_params=PARAMS,
        cost_estimate=FREE,
    )(far(order), far(cache))


def hold_kernel(*refs):
    pass


def hold(arrays, cost):
    count = len(arrays)
    return pl.pallas_call(
        hold_kernel,
        name="hold",
        out_shape=[pltpu.VMEM(array.shape, array.dtype) for array in arrays],
        in_specs=[VMEM] * count,
        out_specs=[VMEM] * count,
        input_output_aliases={n: n for n in range(count)},
        compiler_params=PARAMS,
        cost_estimate=pl.CostEstimate(flops=cost, bytes_accessed=0, transcendentals=0),
    )(*[near(array) for array in arrays])


def fetches(order, cache, swapped, own, other, arrived, chunk):
    groups, first = {}, 0
    base = FIRSTS[chunk] - FIRSTS[1]
    for at, size in enumerate(GROUPS[chunk]):
        copies = [
            pltpu.make_async_copy(
                cache.at[prefill_row(order, FIRSTS[chunk] + n)], own.at[n], arrived.at[n]
            )
            for n in range(first, first + size)
        ]
        if chunk:
            copies.insert(
                0,
                pltpu.make_async_copy(
                    swapped.at[pl.ds(base + first, size)],
                    other.at[pl.ds(first, size)],
                    arrived.at[SIZES[chunk] + at],
                ),
            )
        groups[first] = copies
        first += size
    return groups


def start(groups):
    for copies in groups.values():
        for copy in copies:
            copy.start()


def wait(groups, first):
    for copy in groups.get(first, ()):
        copy.wait()


def held_rows(cache, size):
    return pltpu.VMEM((size, *cache.shape[1:]), cache.dtype)


def arrivals(chunk):
    return pltpu.SemaphoreType.DMA((SIZES[chunk] + len(GROUPS[chunk]),))


def score_kernel(order, lengths, query, cache, swapped, out, own, other, arrived, *, chunk):
    if not chunk:
        other = swapped
    size = SIZES[chunk]
    span = own.shape[1]
    width = 2 * span

    @pl.when(lax.axis_index("head") < 2)
    def _():
        groups = fetches(order, cache, swapped, own, other, arrived, chunk)
        start(groups)
        lane = lax.broadcasted_iota(jnp.int32, (QROWS, LANES), 1)
        column = lax.broadcasted_iota(jnp.int32, (QROWS, span), 1)
        wide = lax.axis_index("wide")
        position = jnp.concatenate([column + wide * span, column + (wide ^ 1) * span], axis=1)
        extra = jnp.zeros((QROWS, LANES), jnp.float32)
        for n in range(size):
            wait(groups, n)
            slot = FIRSTS[chunk] + n
            q = query[slot]
            scores = jnp.concatenate(
                [
                    lax.dot_general(q, own[n], NT, preferred_element_type=jnp.float32),
                    lax.dot_general(q, other[n], NT, preferred_element_type=jnp.float32),
                ],
                axis=1,
            ) * (HD ** (-0.5))
            valid = position < lengths[prefill_row(order, slot)]
            scores = jnp.where(valid, scores, NEGATIVE)
            top = jnp.max(scores, axis=1, keepdims=True)
            top = top.astype(jnp.bfloat16).astype(jnp.float32)
            weights = jnp.where(valid, jnp.exp(scores - top), 0.0)
            total = jnp.sum(weights, axis=1, keepdims=True)
            coarse = total.astype(jnp.bfloat16).astype(jnp.float32)
            out[:, n * width : (n + 1) * width] = weights.astype(out.dtype)
            extra = jnp.where(lane == n, top, extra)
            extra = jnp.where(lane == n + size, coarse, extra)
            extra = jnp.where(lane == n + 2 * size, total - coarse, extra)
        out[:, size * width :] = extra.astype(out.dtype)


def score_rows(order, lengths, query, cache, swapped, chunk):
    size = SIZES[chunk]
    rows = held_rows(cache, size)
    return pl.pallas_call(
        functools.partial(score_kernel, chunk=chunk),
        name="score_rows",
        out_shape=pltpu.VMEM((QROWS, size * 2 * cache.shape[1] + LANES), jnp.bfloat16),
        in_specs=[SMEM, SMEM, VMEM, ANY, ANY if chunk else VMEM],
        out_specs=VMEM,
        scratch_shapes=[rows, rows, arrivals(chunk)],
        compiler_params=PARAMS,
        cost_estimate=FREE,
    )(far(order), far(lengths), near(query), far(cache), (far if chunk else near)(swapped))


LINES = 2 * QROWS
SLAB = 2 * LINES + 16
EXTRAS = 8


def mix_kernel(order, weights, cache, *refs, chunk):
    given, more = chunk > 0, chunk + 1 < CHUNKS
    refs = list(refs)
    own = refs.pop(0) if given else None
    other = refs.pop(0)
    swapped = refs.pop(0) if more else None
    if given:
        refs.pop(0)
    out = refs.pop(0)
    following = [refs.pop(0) for _ in range(2)] if more else []
    if not given:
        own, arrived = refs.pop(0), refs.pop(0)
    if more:
        arrived_next = refs.pop(0)
    made, left = refs
    size = SIZES[chunk]
    span = own.shape[1]
    width = 2 * span

    @pl.when(lax.axis_index("head") >= 2)
    def _():
        if not given:
            groups = fetches(order, cache, None, own, other, arrived, chunk)
            start(groups)
        if more:
            groups_next = fetches(order, cache, swapped, *following, arrived_next, chunk + 1)
            start(groups_next)
        extra = weights[:, size * width :].astype(jnp.float32)
        extra = jnp.concatenate([extra, jnp.zeros((LANES - QROWS, LANES), jnp.float32)], axis=0)
        extra = jnp.transpose(extra)
        blank = jnp.zeros((16 - 6, LANES), jnp.float32)
        for pair in range(size // 2):
            if not given:
                wait(groups, 2 * pair)
            rows, lines = [], []
            for n in (2 * pair, 2 * pair + 1):
                at = n * width
                rows.append(
                    jnp.dot(
                        weights[:, at : at + span], own[n], preferred_element_type=jnp.float32
                    )
                    + jnp.dot(
                        weights[:, at + span : at + width],
                        other[n],
                        preferred_element_type=jnp.float32,
                    )
                )
                lines += [extra[n + k * size : n + k * size + 1] for k in range(3)]
            slab = [row[:, :LANES] for row in rows] + [row[:, LANES:] for row in rows]
            made[pair] = jnp.concatenate([*slab, *lines, blank], axis=0).astype(made.dtype)
        copy = pltpu.make_async_copy(
            made, out.at[pl.ds(FIRSTS[chunk] // 2, size // 2)], left.at[0]
        )
        copy.start()
        copy.wait()
        if more:
            for first in groups_next:
                wait(groups_next, first)


def mix_rows(order, weights, cache, swapped, chunk, before, rows, cost):
    given, more = chunk > 0, chunk + 1 < CHUNKS
    size = SIZES[chunk]
    payload = pltpu.HBM((SLOTS // 2, SLAB, LANES), jnp.bfloat16)
    in_specs = [SMEM, VMEM, ANY]
    operands = [far(order), near(weights), far(cache)]
    for array in rows if given else [swapped[chunk]]:
        in_specs.append(VMEM)
        operands.append(near(array))
    if more:
        in_specs.append(ANY)
        operands.append(far(swapped[chunk + 1]))
    aliases = {}
    if given:
        in_specs.append(ANY)
        aliases = {len(operands): 0}
        operands.append(far(before))
    following = [held_rows(cache, SIZES[chunk + 1])] * 2 if more else []
    made = pl.pallas_call(
        functools.partial(mix_kernel, chunk=chunk),
        name="mix_rows",
        out_shape=[payload, *following],
        in_specs=in_specs,
        out_specs=[ANY] + [VMEM] * len(following),
        input_output_aliases=aliases,
        scratch_shapes=([] if given else [held_rows(cache, size), arrivals(chunk)])
        + ([arrivals(chunk + 1)] if more else [])
        + [pltpu.VMEM((size // 2, SLAB, LANES), jnp.bfloat16), pltpu.SemaphoreType.DMA((1,))],
        compiler_params=PARAMS,
        cost_estimate=pl.CostEstimate(flops=cost, bytes_accessed=0, transcendentals=0),
    )(*operands)
    return made[0], made[1:]


def combine_kernel(parts, query, fresh, low, high):
    @pl.when(lax.axis_index("head") >= 2)
    def _():
        chips = parts.shape[0]
        second = lax.axis_index("head") & 1
        half = KVH * HD
        extras = jnp.stack(
            [parts[chip, 2 * LINES :].astype(jnp.float32)[:EXTRAS] for chip in range(chips)]
        )
        tops = [extras[:, 3 * row] for row in range(2)]
        totals = [extras[:, 3 * row + 1] + extras[:, 3 * row + 2] for row in range(2)]
        step = lax.broadcasted_iota(jnp.int32, (QROWS, STEPS), 0) // GROUP
        time = lax.broadcasted_iota(jnp.int32, (QROWS, STEPS), 1)
        keep = time <= step
        scores, values = [], []
        for row in range(2):
            news = fresh[row].astype(jnp.float32)
            keys = jnp.where(second == 1, news[:, HD:half], news[:, :HD])
            values.append(jnp.where(second == 1, news[:, half + HD :], news[:, half : half + HD]))
            q = jnp.where(second == 1, query[row, :, GROUP:], query[row, :, :GROUP])
            q = q.reshape(QROWS, HD).astype(jnp.float32)
            columns = [
                jnp.sum(q * keys[t : t + 1], axis=1, keepdims=True) for t in range(STEPS)
            ]
            score = jnp.concatenate(columns, axis=1) * (HD ** (-0.5))
            scores.append(jnp.where(keep, score, NEGATIVE))
        lines, marks = [], []
        for row in range(2):
            top = jnp.max(tops[row], axis=0, keepdims=True)
            factors = jnp.exp(tops[row] - top)
            lines += [top, jnp.sum(factors * totals[row], axis=0, keepdims=True)]
            marks.append(factors)
        blank = jnp.zeros((LANES - 4 - 2 * chips, LANES), jnp.float32)
        columns = jnp.transpose(jnp.concatenate([*marks, *lines, blank], axis=0))[:QROWS]
        halves = []
        for row in range(2):
            at = 2 * chips + 2 * row
            cached = columns[:, at : at + 1]
            top = jnp.maximum(cached, jnp.max(scores[row], axis=1, keepdims=True))
            scale = jnp.exp(cached - top)
            probs = jnp.where(keep, jnp.exp(scores[row] - top), 0.0)
            total = columns[:, at + 1 : at + 2] * scale + jnp.sum(probs, axis=1, keepdims=True)
            probs = probs.astype(jnp.bfloat16).astype(jnp.float32)
            mixed = sum(probs[:, t : t + 1] * values[row][t : t + 1] for t in range(STEPS))
            first = row * QROWS
            sides = []
            for k in range(2):
                acc = jnp.zeros((QROWS, LANES), jnp.float32)
                for chip in range(chips):
                    span = slice(k * LINES + first, k * LINES + first + QROWS)
                    part = parts[chip, span].astype(jnp.float32)
                    at = row * chips + chip
                    acc = acc + columns[:, at : at + 1] * part
                sides.append(acc * scale + mixed[:, k * LANES : (k + 1) * LANES])
            halves.append(jnp.concatenate(sides, axis=1) / total)
        heads = GROUP // 2
        for row in range(2):
            for s in range(STEPS):
                for a in range(heads):
                    at = s * GROUP + a
                    span = slice(a * HD, (a + 1) * HD)
                    low[s, row : row + 1, span] = halves[row][at : at + 1]
                    high[s, row : row + 1, span] = halves[row][at + heads : at + heads + 1]


def combine(parts, query, fresh):
    heads = GROUP // 2
    shape = pltpu.VMEM((STEPS, 2, heads * HD), jnp.float32)
    return pl.pallas_call(
        combine_kernel,
        name="combine_parts",
        out_shape=(shape, shape),
        in_specs=[VMEM, VMEM, VMEM],
        out_specs=(VMEM, VMEM),
        compiler_params=PARAMS,
        cost_estimate=FREE,
    )(near(parts), near(query), near(fresh))


NEAR = 4


def block_kernel(*refs, moves):
    for target, at, source, place in moves:
        refs[target][at] = refs[source][place].astype(refs[target].dtype)


def move_blocks(name, arrays, shapes, moves):
    count = len(arrays)
    return pl.pallas_call(
        functools.partial(
            block_kernel, moves=[(count + t, at, source, place) for t, at, source, place in moves]
        ),
        name=name,
        out_shape=[pltpu.VMEM(shape, jnp.bfloat16) for shape in shapes],
        in_specs=[VMEM] * count,
        out_specs=[VMEM] * len(shapes),
        compiler_params=PARAMS,
        cost_estimate=FREE,
    )(*[near(array) for array in arrays])


def split_kernel(order, states, mine, theirs):
    wide = lax.axis_index("wide")
    for z in range(NEAR):
        for y in range(NEAR):
            chip = (wide >> 1) ^ (4 * y + z)
            for row in range(2):
                at = 4 * chip + 2 * (wide & 1) + row
                mine[z, y, row] = states[order[at]].astype(mine.dtype)
                theirs[z, y, row] = states[order[at ^ 2]].astype(theirs.dtype)


def split_states(order, states):
    shape = pltpu.VMEM((NEAR, NEAR, 2, *states.shape[1:]), jnp.bfloat16)
    return pl.pallas_call(
        split_kernel,
        name="split_states",
        out_shape=(shape, shape),
        in_specs=[SMEM, VMEM],
        out_specs=(VMEM, VMEM),
        compiler_params=PARAMS,
        cost_estimate=FREE,
    )(far(order), near(states))


def along_z(mine, other):
    shape = (2, *mine.shape[1:])
    moves = [(z, core, core, z) for z in range(NEAR) for core in range(2)]
    return move_blocks("pack_z", [mine, other], [shape] * NEAR, moves)


def along_y(blocks):
    shape = (NEAR, 2, *blocks[0].shape[2:])
    moves = [
        (y, (z, core), z, (core, y)) for y in range(NEAR) for z in range(NEAR) for core in range(2)
    ]
    return move_blocks("pack_y", blocks, [shape] * NEAR, moves)


def join_kernel(*refs):
    blocks, out = refs[:NEAR], refs[NEAR]
    wide = lax.axis_index("wide")
    for y in range(NEAR):
        for z in range(NEAR):
            for core in range(2):
                out[wide ^ (8 * y + 2 * z + core)] = blocks[y][z, core]


def join_states(blocks):
    shape = (2 * NEAR * NEAR, *blocks[0].shape[2:])
    return pl.pallas_call(
        join_kernel,
        name="join_states",
        out_shape=pltpu.VMEM(shape, jnp.bfloat16),
        in_specs=[VMEM] * NEAR,
        out_specs=VMEM,
        compiler_params=PARAMS,
        cost_estimate=FREE,
    )(*[near(block) for block in blocks])


def delta_kernel(decay, beta, states, query, key, value, gate, out, final, rows):
    batch, steps, heads_k, width = key.shape
    heads_v = value.shape[2]
    ratio = heads_v // heads_k
    keys_at = batch * steps * heads_k

    def column(row, step, head):
        return (row * steps + step) * heads_k + head

    rows[...] = jnp.zeros_like(rows)
    for row in range(batch):
        for step in range(steps):
            at = column(row, step, 0)
            q = query[row, step].astype(jnp.float32)
            k = key[row, step].astype(jnp.float32)
            q = q * lax.rsqrt(jnp.sum(q * q, -1, keepdims=True) + 1e-06) * width ** (-0.5)
            k = k * lax.rsqrt(jnp.sum(k * k, -1, keepdims=True) + 1e-06)
            rows[at : at + heads_k] = q
            rows[keys_at + at : keys_at + at + heads_k] = k
    columns = jnp.transpose(rows[...])
    shape = (width, value.shape[3])
    for row in range(batch):
        made = [[] for _ in range(steps)]
        values = [value[row, step].astype(jnp.float32) for step in range(steps)]
        for head in range(heads_k):
            both = range(head * ratio, (head + 1) * ratio)
            held = [states[row, one].astype(jnp.float32) for one in both]
            for step in range(steps):
                at = column(row, step, head)
                q = jnp.broadcast_to(columns[:, at : at + 1], shape)
                k = jnp.broadcast_to(columns[:, keys_at + at : keys_at + at + 1], shape)
                for n, one in enumerate(both):
                    rate = decay[row, step, one]
                    recalled = jnp.sum(k * held[n], axis=0, keepdims=True)
                    change = beta[row, step, one] * (
                        values[step][one : one + 1] - rate * recalled
                    )
                    held[n] = rate * held[n] + k * change
                    made[step].append(jnp.sum(q * held[n], axis=0, keepdims=True))
            for n, one in enumerate(both):
                final[row, one] = held[n]
        for step in range(steps):
            read = jnp.concatenate(made[step], axis=0)
            read = read * lax.rsqrt(jnp.mean(read * read, -1, keepdims=True) + 1e-06)
            level = gate[row, step].astype(jnp.float32)
            out[row, step] = (read * (level * jax.nn.sigmoid(level))).astype(out.dtype)


def delta_rule(states, query, key, value, decay, beta, gate):
    width = key.shape[-1]
    return pl.pallas_call(
        delta_kernel,
        name="delta_rule",
        out_shape=(
            jax.ShapeDtypeStruct(value.shape, jnp.bfloat16),
            jax.ShapeDtypeStruct(states.shape, jnp.float32),
        ),
        in_specs=[SMEM, SMEM] + [VMEM] * 5,
        out_specs=(VMEM, VMEM),
        scratch_shapes=[pltpu.VMEM((width, width), jnp.float32)],
        compiler_params=PARAMS,
        cost_estimate=FREE,
    )(decay, beta, states, query, key, value, gate)


def on_device(
    kv_cache,
    lin_states,
    row_order,
    prompt_lengths,
    att_query,
    new_kv,
    att_gate,
    lin_query,
    lin_key,
    lin_value,
    lin_decay,
    lin_beta,
    lin_gate,
):
    wide_count = lax.axis_size("wide")
    chips = wide_count // 2
    head_index = lax.axis_index("head")
    def across(array, distance=1):
        pairs = [(i, i ^ distance) for i in range(wide_count)]
        return lax.ppermute(array, "wide", pairs)

    def after(array, *others):
        return lax.optimization_barrier((array, *others))[0]

    same_core = [[2 * k + c for k in range(chips)] for c in range(2)]

    def between_chips(array):
        return lax.all_to_all(array, "wide", 0, 0, tiled=True, axis_index_groups=same_core)

    sides = [
        jnp.broadcast_to(side.reshape(1, 2, QROWS, HD), (chips, 2, QROWS, HD))
        for side in (att_query[:, :, :GROUP], att_query[:, :, GROUP:])
    ]
    copies = jnp.where(head_index % KVH == 1, sides[1], sides[0])
    (query,) = hold([between_chips(copies.reshape(2 * chips, QROWS, HD))], 30 * 10**9)

    first = gather_rows(row_order, kv_cache, 0, FIRSTS[1])
    made = [first, gather_rows(after(row_order, first), kv_cache, FIRSTS[1], SLOTS - FIRSTS[1])]
    rows_all, heads, depth, width = lin_states.shape
    mine, theirs = split_states(
        after(row_order, *made), lin_states.reshape(rows_all, heads * depth, width)
    )
    query, first = hold([query, across(made[0])], 30 * 10**9)
    swapped = [first] + [across(made[1])] * (CHUNKS - 1)
    (other,) = hold([across(theirs)], 30 * 10**9)

    weights = []
    for chunk in range(CHUNKS):
        order = after(row_order, theirs, *weights)
        weights.append(
            score_rows(order, prompt_lengths, query, kv_cache, swapped[chunk], chunk)
        )
    moved = [lax.ppermute(made, "head", [(0, 2), (1, 3)]) for made in weights]

    blocks = along_z(after(mine, weights[-1]), other)
    crossed = [across(block, 2 * z) for z, block in enumerate(blocks[1:], 1)]
    blocks = [blocks[0], *hold(crossed, 10 * 10**9)]
    payload, rows = None, None
    for chunk in range(CHUNKS):
        cost = 10 * 10**9 if chunk + 1 == CHUNKS else 3 * 10**9
        payload, rows = mix_rows(
            after(row_order, weights[-1]), moved[chunk], kv_cache, swapped, chunk, payload, rows,
            cost,
        )
    parts = between_chips(payload)
    blocks = along_y([after(blocks[0], payload), *blocks[1:]])
    blocks = [blocks[0]] + [across(block, 8 * y) for y, block in enumerate(blocks[1:], 1)]
    low, high = combine(parts, att_query, new_kv)
    states = join_states([after(blocks[0], low), *blocks[1:]])
    states = states.reshape(wide_count, 2, heads, depth, width)
    states = states.transpose(1, 2, 0, 3, 4).reshape(2, heads, wide_count * depth, width)
    lin_out, final_states = delta_rule(
        states, lin_query, lin_key, lin_value, lin_decay, lin_beta, lin_gate
    )
    low_here = lax.ppermute(low, "head", [(2, 0), (3, 2)])
    high_here = lax.ppermute(high, "head", [(2, 1)])
    result = jnp.where(
        head_index == 3, high, jnp.where(head_index == 1, high_here, low_here)
    )
    gate = jnp.transpose(att_gate, (1, 0, 2)).astype(jnp.float32)
    att_out = (result * jax.nn.sigmoid(gate)).astype(jnp.bfloat16)
    att_out = jnp.transpose(att_out, (1, 0, 2))
    return (att_out, lin_out, final_states)


def solution(mesh):
    placed = (
        P(None, "wide", "head"),
        P(None, "head", "wide", None),
        P(),
        P(),
        P("wide", None, None, None),
        P("wide", None, None),
        P("wide", None, "head"),
        P("wide", None, "head", None),
        P("wide", None, "head", None),
        P("wide", None, "head", None),
        P("wide", None, "head"),
        P("wide", None, "head"),
        P("wide", None, "head", None),
    )
    return jax.shard_map(
        on_device,
        mesh=mesh,
        in_specs=placed,
        out_specs=(
            P("wide", None, "head"),
            P("wide", None, "head", None),
            P("wide", "head", None, None),
        ),
        check_vma=False,
    )
```

```python
import functools

import jax
import jax.numpy as jnp
from jax import lax
from jax.experimental import pallas as pl
from jax.experimental.pallas import tpu as pltpu
from jax.sharding import PartitionSpec as P

HQ = 16
KVH = 2
HD = 256
STEPS = 3
GROUP = HQ // KVH
QROWS = STEPS * GROUP
LANES = 128
NEGATIVE = -1e30

SLOTS = 32
SIZES = (12, 12, 8)
FIRSTS = (0, 12, 24)
CHUNKS = 3
GROUPS = ((4, 8), (4, 8), (8,))
NT = (((1,), (1,)), ((), ()))
LIMIT = 16 * 2**20
VMEM = pl.BlockSpec(memory_space=pltpu.VMEM)
SMEM = pl.BlockSpec(memory_space=pltpu.SMEM)
ANY = pl.BlockSpec(memory_space=pltpu.HBM)
PARAMS = pltpu.CompilerParams(vmem_limit_bytes=LIMIT)
FREE = pl.CostEstimate(flops=0, bytes_accessed=0, transcendentals=0)

def near(array):
    return pltpu.with_memory_space_constraint(array, pltpu.VMEM)


def far(array):
    return pltpu.with_memory_space_constraint(array, pltpu.HBM)


def prefill_row(order, slot, other=0):
    core = (lax.axis_index("wide") & 1) ^ other
    return order[4 * (slot // 2) + 2 * core + slot % 2]


def gather_kernel(order, cache, out, held, arrived, left, *, first):
    count = out.shape[0]
    reads = [
        pltpu.make_async_copy(cache.at[prefill_row(order, first + n, 1)], held.at[n], arrived.at[n])
        for n in range(count)
    ]
    writes = [pltpu.make_async_copy(held.at[n], out.at[n], left.at[n]) for n in range(count)]
    for read in reads:
        read.start()
    for read, write in zip(reads, writes):
        read.wait()
        write.start()
    for write in writes:
        write.wait()


def gather_rows(order, cache, first, count):
    copies = pltpu.SemaphoreType.DMA((count,))
    return pl.pallas_call(
        functools.partial(gather_kernel, first=first),
        name="gather_rows",
        out_shape=pltpu.HBM((count, *cache.shape[1:]), cache.dtype),
        in_specs=[SMEM, ANY],
        out_specs=ANY,
        scratch_shapes=[held_rows(cache, count), copies, copies],
        compiler_params=PARAMS,
        cost_estimate=FREE,
    )(far(order), far(cache))


def hold_kernel(*refs):
    pass


def hold(arrays, cost):
    count = len(arrays)
    return pl.pallas_call(
        hold_kernel,
        name="hold",
        out_shape=[pltpu.VMEM(array.shape, array.dtype) for array in arrays],
        in_specs=[VMEM] * count,
        out_specs=[VMEM] * count,
        input_output_aliases={n: n for n in range(count)},
        compiler_params=PARAMS,
        cost_estimate=pl.CostEstimate(flops=cost, bytes_accessed=0, transcendentals=0),
    )(*[near(array) for array in arrays])


def fetches(order, cache, swapped, own, other, arrived, chunk):
    groups, first = {}, 0
    base = FIRSTS[chunk] - FIRSTS[1]
    for at, size in enumerate(GROUPS[chunk]):
        copies = [
            pltpu.make_async_copy(
                cache.at[prefill_row(order, FIRSTS[chunk] + n)], own.at[n], arrived.at[n]
            )
            for n in range(first, first + size)
        ]
        if chunk:
            copies.insert(
                0,
                pltpu.make_async_copy(
                    swapped.at[pl.ds(base + first, size)],
                    other.at[pl.ds(first, size)],
                    arrived.at[SIZES[chunk] + at],
                ),
            )
        groups[first] = copies
        first += size
    return groups


def start(groups):
    for copies in groups.values():
        for copy in copies:
            copy.start()


def wait(groups, first):
    for copy in groups.get(first, ()):
        copy.wait()


def held_rows(cache, size):
    return pltpu.VMEM((size, *cache.shape[1:]), cache.dtype)


def arrivals(chunk):
    return pltpu.SemaphoreType.DMA((SIZES[chunk] + len(GROUPS[chunk]),))


def score_kernel(order, lengths, query, cache, swapped, out, own, other, arrived, *, chunk):
    if not chunk:
        other = swapped
    size = SIZES[chunk]
    span = own.shape[1]
    width = 2 * span

    @pl.when(lax.axis_index("head") < 2)
    def _():
        groups = fetches(order, cache, swapped, own, other, arrived, chunk)
        start(groups)
        lane = lax.broadcasted_iota(jnp.int32, (QROWS, LANES), 1)
        column = lax.broadcasted_iota(jnp.int32, (QROWS, span), 1)
        wide = lax.axis_index("wide")
        position = jnp.concatenate([column + wide * span, column + (wide ^ 1) * span], axis=1)
        extra = jnp.zeros((QROWS, LANES), jnp.float32)
        for n in range(size):
            wait(groups, n)
            slot = FIRSTS[chunk] + n
            q = query[slot]
            scores = jnp.concatenate(
                [
                    lax.dot_general(q, own[n], NT, preferred_element_type=jnp.float32),
                    lax.dot_general(q, other[n], NT, preferred_element_type=jnp.float32),
                ],
                axis=1,
            ) * (HD ** (-0.5))
            valid = position < lengths[prefill_row(order, slot)]
            scores = jnp.where(valid, scores, NEGATIVE)
            top = jnp.max(scores, axis=1, keepdims=True)
            top = top.astype(jnp.bfloat16).astype(jnp.float32)
            weights = jnp.where(valid, jnp.exp(scores - top), 0.0)
            total = jnp.sum(weights, axis=1, keepdims=True)
            coarse = total.astype(jnp.bfloat16).astype(jnp.float32)
            out[:, n * width : (n + 1) * width] = weights.astype(out.dtype)
            extra = jnp.where(lane == n, top, extra)
            extra = jnp.where(lane == n + size, coarse, extra)
            extra = jnp.where(lane == n + 2 * size, total - coarse, extra)
        out[:, size * width :] = extra.astype(out.dtype)


def score_rows(order, lengths, query, cache, swapped, chunk):
    size = SIZES[chunk]
    rows = held_rows(cache, size)
    return pl.pallas_call(
        functools.partial(score_kernel, chunk=chunk),
        name="score_rows",
        out_shape=pltpu.VMEM((QROWS, size * 2 * cache.shape[1] + LANES), jnp.bfloat16),
        in_specs=[SMEM, SMEM, VMEM, ANY, ANY if chunk else VMEM],
        out_specs=VMEM,
        scratch_shapes=[rows, rows, arrivals(chunk)],
        compiler_params=PARAMS,
        cost_estimate=FREE,
    )(far(order), far(lengths), near(query), far(cache), (far if chunk else near)(swapped))


LINES = 2 * QROWS
SLAB = 2 * LINES + 16
EXTRAS = 8


def mix_kernel(order, weights, cache, *refs, chunk):
    given, more = chunk > 0, chunk + 1 < CHUNKS
    refs = list(refs)
    own = refs.pop(0) if given else None
    other = refs.pop(0)
    swapped = refs.pop(0) if more else None
    if given:
        refs.pop(0)
    out = refs.pop(0)
    following = [refs.pop(0) for _ in range(2)] if more else []
    if not given:
        own, arrived = refs.pop(0), refs.pop(0)
    if more:
        arrived_next = refs.pop(0)
    made, left = refs
    size = SIZES[chunk]
    span = own.shape[1]
    width = 2 * span

    @pl.when(lax.axis_index("head") >= 2)
    def _():
        if not given:
            groups = fetches(order, cache, None, own, other, arrived, chunk)
            start(groups)
        if more:
            groups_next = fetches(order, cache, swapped, *following, arrived_next, chunk + 1)
            start(groups_next)
        extra = weights[:, size * width :].astype(jnp.float32)
        extra = jnp.concatenate([extra, jnp.zeros((LANES - QROWS, LANES), jnp.float32)], axis=0)
        extra = jnp.transpose(extra)
        blank = jnp.zeros((16 - 6, LANES), jnp.float32)
        for pair in range(size // 2):
            if not given:
                wait(groups, 2 * pair)
            rows, lines = [], []
            for n in (2 * pair, 2 * pair + 1):
                at = n * width
                rows.append(
                    jnp.dot(
                        weights[:, at : at + span], own[n], preferred_element_type=jnp.float32
                    )
                    + jnp.dot(
                        weights[:, at + span : at + width],
                        other[n],
                        preferred_element_type=jnp.float32,
                    )
                )
                lines += [extra[n + k * size : n + k * size + 1] for k in range(3)]
            slab = [row[:, :LANES] for row in rows] + [row[:, LANES:] for row in rows]
            made[pair] = jnp.concatenate([*slab, *lines, blank], axis=0).astype(made.dtype)
        copy = pltpu.make_async_copy(
            made, out.at[pl.ds(FIRSTS[chunk] // 2, size // 2)], left.at[0]
        )
        copy.start()
        copy.wait()
        if more:
            for first in groups_next:
                wait(groups_next, first)


def mix_rows(order, weights, cache, swapped, chunk, before, rows, cost):
    given, more = chunk > 0, chunk + 1 < CHUNKS
    size = SIZES[chunk]
    payload = pltpu.HBM((SLOTS // 2, SLAB, LANES), jnp.bfloat16)
    in_specs = [SMEM, VMEM, ANY]
    operands = [far(order), near(weights), far(cache)]
    for array in rows if given else [swapped[chunk]]:
        in_specs.append(VMEM)
        operands.append(near(array))
    if more:
        in_specs.append(ANY)
        operands.append(far(swapped[chunk + 1]))
    aliases = {}
    if given:
        in_specs.append(ANY)
        aliases = {len(operands): 0}
        operands.append(far(before))
    following = [held_rows(cache, SIZES[chunk + 1])] * 2 if more else []
    made = pl.pallas_call(
        functools.partial(mix_kernel, chunk=chunk),
        name="mix_rows",
        out_shape=[payload, *following],
        in_specs=in_specs,
        out_specs=[ANY] + [VMEM] * len(following),
        input_output_aliases=aliases,
        scratch_shapes=([] if given else [held_rows(cache, size), arrivals(chunk)])
        + ([arrivals(chunk + 1)] if more else [])
        + [pltpu.VMEM((size // 2, SLAB, LANES), jnp.bfloat16), pltpu.SemaphoreType.DMA((1,))],
        compiler_params=PARAMS,
        cost_estimate=pl.CostEstimate(flops=cost, bytes_accessed=0, transcendentals=0),
    )(*operands)
    return made[0], made[1:]


def combine_kernel(parts, query, fresh, low, high):
    @pl.when(lax.axis_index("head") >= 2)
    def _():
        chips = parts.shape[0]
        second = lax.axis_index("head") & 1
        half = KVH * HD
        extras = jnp.stack(
            [parts[chip, 2 * LINES :].astype(jnp.float32)[:EXTRAS] for chip in range(chips)]
        )
        tops = [extras[:, 3 * row] for row in range(2)]
        totals = [extras[:, 3 * row + 1] + extras[:, 3 * row + 2] for row in range(2)]
        step = lax.broadcasted_iota(jnp.int32, (QROWS, STEPS), 0) // GROUP
        time = lax.broadcasted_iota(jnp.int32, (QROWS, STEPS), 1)
        keep = time <= step
        scores, values = [], []
        for row in range(2):
            news = fresh[row].astype(jnp.float32)
            keys = jnp.where(second == 1, news[:, HD:half], news[:, :HD])
            values.append(jnp.where(second == 1, news[:, half + HD :], news[:, half : half + HD]))
            q = jnp.where(second == 1, query[row, :, GROUP:], query[row, :, :GROUP])
            q = q.reshape(QROWS, HD).astype(jnp.float32)
            columns = [
                jnp.sum(q * keys[t : t + 1], axis=1, keepdims=True) for t in range(STEPS)
            ]
            score = jnp.concatenate(columns, axis=1) * (HD ** (-0.5))
            scores.append(jnp.where(keep, score, NEGATIVE))
        lines, marks = [], []
        for row in range(2):
            top = jnp.max(tops[row], axis=0, keepdims=True)
            factors = jnp.exp(tops[row] - top)
            lines += [top, jnp.sum(factors * totals[row], axis=0, keepdims=True)]
            marks.append(factors)
        blank = jnp.zeros((LANES - 4 - 2 * chips, LANES), jnp.float32)
        columns = jnp.transpose(jnp.concatenate([*marks, *lines, blank], axis=0))[:QROWS]
        halves = []
        for row in range(2):
            at = 2 * chips + 2 * row
            cached = columns[:, at : at + 1]
            top = jnp.maximum(cached, jnp.max(scores[row], axis=1, keepdims=True))
            scale = jnp.exp(cached - top)
            probs = jnp.where(keep, jnp.exp(scores[row] - top), 0.0)
            total = columns[:, at + 1 : at + 2] * scale + jnp.sum(probs, axis=1, keepdims=True)
            probs = probs.astype(jnp.bfloat16).astype(jnp.float32)
            mixed = sum(probs[:, t : t + 1] * values[row][t : t + 1] for t in range(STEPS))
            first = row * QROWS
            sides = []
            for k in range(2):
                acc = jnp.zeros((QROWS, LANES), jnp.float32)
                for chip in range(chips):
                    span = slice(k * LINES + first, k * LINES + first + QROWS)
                    part = parts[chip, span].astype(jnp.float32)
                    at = row * chips + chip
                    acc = acc + columns[:, at : at + 1] * part
                sides.append(acc * scale + mixed[:, k * LANES : (k + 1) * LANES])
            halves.append(jnp.concatenate(sides, axis=1) / total)
        heads = GROUP // 2
        for row in range(2):
            for s in range(STEPS):
                for a in range(heads):
                    at = s * GROUP + a
                    span = slice(a * HD, (a + 1) * HD)
                    low[s, row : row + 1, span] = halves[row][at : at + 1]
                    high[s, row : row + 1, span] = halves[row][at + heads : at + heads + 1]


def combine(parts, query, fresh):
    heads = GROUP // 2
    shape = pltpu.VMEM((STEPS, 2, heads * HD), jnp.float32)
    return pl.pallas_call(
        combine_kernel,
        name="combine_parts",
        out_shape=(shape, shape),
        in_specs=[VMEM, VMEM, VMEM],
        out_specs=(VMEM, VMEM),
        compiler_params=PARAMS,
        cost_estimate=FREE,
    )(near(parts), near(query), near(fresh))


NEAR = 4


def block_kernel(*refs, moves):
    for target, at, source, place in moves:
        refs[target][at] = refs[source][place].astype(refs[target].dtype)


def move_blocks(name, arrays, shapes, moves):
    count = len(arrays)
    return pl.pallas_call(
        functools.partial(
            block_kernel, moves=[(count + t, at, source, place) for t, at, source, place in moves]
        ),
        name=name,
        out_shape=[pltpu.VMEM(shape, jnp.bfloat16) for shape in shapes],
        in_specs=[VMEM] * count,
        out_specs=[VMEM] * len(shapes),
        compiler_params=PARAMS,
        cost_estimate=FREE,
    )(*[near(array) for array in arrays])


def split_kernel(order, states, mine, theirs):
    wide = lax.axis_index("wide")
    for z in range(NEAR):
        for y in range(NEAR):
            chip = (wide >> 1) ^ (4 * y + z)
            for row in range(2):
                at = 4 * chip + 2 * (wide & 1) + row
                mine[z, y, row] = states[order[at]].astype(mine.dtype)
                theirs[z, y, row] = states[order[at ^ 2]].astype(theirs.dtype)


def split_states(order, states):
    shape = pltpu.VMEM((NEAR, NEAR, 2, *states.shape[1:]), jnp.bfloat16)
    return pl.pallas_call(
        split_kernel,
        name="split_states",
        out_shape=(shape, shape),
        in_specs=[SMEM, VMEM],
        out_specs=(VMEM, VMEM),
        compiler_params=PARAMS,
        cost_estimate=FREE,
    )(far(order), near(states))


def along_z(mine, other):
    shape = (2, *mine.shape[1:])
    moves = [(z, core, core, z) for z in range(NEAR) for core in range(2)]
    return move_blocks("pack_z", [mine, other], [shape] * NEAR, moves)


def along_y(blocks):
    shape = (NEAR, 2, *blocks[0].shape[2:])
    moves = [
        (y, (z, core), z, (core, y)) for y in range(NEAR) for z in range(NEAR) for core in range(2)
    ]
    return move_blocks("pack_y", blocks, [shape] * NEAR, moves)


def join_kernel(*refs):
    blocks, out = refs[:NEAR], refs[NEAR]
    wide = lax.axis_index("wide")
    for y in range(NEAR):
        for z in range(NEAR):
            for core in range(2):
                out[wide ^ (8 * y + 2 * z + core)] = blocks[y][z, core]


def join_states(blocks):
    shape = (2 * NEAR * NEAR, *blocks[0].shape[2:])
    return pl.pallas_call(
        join_kernel,
        name="join_states",
        out_shape=pltpu.VMEM(shape, jnp.bfloat16),
        in_specs=[VMEM] * NEAR,
        out_specs=VMEM,
        compiler_params=PARAMS,
        cost_estimate=FREE,
    )(*[near(block) for block in blocks])


def delta_kernel(decay, beta, states, query, key, value, gate, out, final, rows):
    batch, steps, heads_k, width = key.shape
    heads_v = value.shape[2]
    ratio = heads_v // heads_k
    keys_at = batch * steps * heads_k

    def column(row, step, head):
        return (row * steps + step) * heads_k + head

    rows[...] = jnp.zeros_like(rows)
    for row in range(batch):
        for step in range(steps):
            at = column(row, step, 0)
            q = query[row, step].astype(jnp.float32)
            k = key[row, step].astype(jnp.float32)
            q = q * lax.rsqrt(jnp.sum(q * q, -1, keepdims=True) + 1e-06) * width ** (-0.5)
            k = k * lax.rsqrt(jnp.sum(k * k, -1, keepdims=True) + 1e-06)
            rows[at : at + heads_k] = q
            rows[keys_at + at : keys_at + at + heads_k] = k
    columns = jnp.transpose(rows[...])
    shape = (width, value.shape[3])
    for row in range(batch):
        made = [[] for _ in range(steps)]
        values = [value[row, step].astype(jnp.float32) for step in range(steps)]
        for head in range(heads_k):
            both = range(head * ratio, (head + 1) * ratio)
            held = [states[row, one].astype(jnp.float32) for one in both]
            for step in range(steps):
                at = column(row, step, head)
                q = jnp.broadcast_to(columns[:, at : at + 1], shape)
                k = jnp.broadcast_to(columns[:, keys_at + at : keys_at + at + 1], shape)
                for n, one in enumerate(both):
                    rate = decay[row, step, one]
                    recalled = jnp.sum(k * held[n], axis=0, keepdims=True)
                    change = beta[row, step, one] * (
                        values[step][one : one + 1] - rate * recalled
                    )
                    held[n] = rate * held[n] + k * change
                    made[step].append(jnp.sum(q * held[n], axis=0, keepdims=True))
            for n, one in enumerate(both):
                final[row, one] = held[n]
        for step in range(steps):
            read = jnp.concatenate(made[step], axis=0)
            read = read * lax.rsqrt(jnp.mean(read * read, -1, keepdims=True) + 1e-06)
            level = gate[row, step].astype(jnp.float32)
            out[row, step] = (read * (level * jax.nn.sigmoid(level))).astype(out.dtype)


def delta_rule(states, query, key, value, decay, beta, gate):
    width = key.shape[-1]
    return pl.pallas_call(
        delta_kernel,
        name="delta_rule",
        out_shape=(
            jax.ShapeDtypeStruct(value.shape, jnp.bfloat16),
            jax.ShapeDtypeStruct(states.shape, jnp.float32),
        ),
        in_specs=[SMEM, SMEM] + [VMEM] * 5,
        out_specs=(VMEM, VMEM),
        scratch_shapes=[pltpu.VMEM((width, width), jnp.float32)],
        compiler_params=PARAMS,
        cost_estimate=FREE,
    )(decay, beta, states, query, key, value, gate)


def on_device(
    kv_cache,
    lin_states,
    row_order,
    prompt_lengths,
    att_query,
    new_kv,
    att_gate,
    lin_query,
    lin_key,
    lin_value,
    lin_decay,
    lin_beta,
    lin_gate,
):
    wide_count = lax.axis_size("wide")
    chips = wide_count // 2
    head_index = lax.axis_index("head")
    def across(array, distance=1):
        pairs = [(i, i ^ distance) for i in range(wide_count)]
        return lax.ppermute(array, "wide", pairs)

    def after(array, *others):
        return lax.optimization_barrier((array, *others))[0]

    same_core = [[2 * k + c for k in range(chips)] for c in range(2)]

    def between_chips(array):
        return lax.all_to_all(array, "wide", 0, 0, tiled=True, axis_index_groups=same_core)

    sides = [
        jnp.broadcast_to(side.reshape(1, 2, QROWS, HD), (chips, 2, QROWS, HD))
        for side in (att_query[:, :, :GROUP], att_query[:, :, GROUP:])
    ]
    copies = jnp.where(head_index % KVH == 1, sides[1], sides[0])
    (query,) = hold([between_chips(copies.reshape(2 * chips, QROWS, HD))], 30 * 10**9)

    first = gather_rows(row_order, kv_cache, 0, FIRSTS[1])
    made = [first, gather_rows(after(row_order, first), kv_cache, FIRSTS[1], SLOTS - FIRSTS[1])]
    rows_all, heads, depth, width = lin_states.shape
    mine, theirs = split_states(
        after(row_order, *made), lin_states.reshape(rows_all, heads * depth, width)
    )
    query, first = hold([query, across(made[0])], 30 * 10**9)
    swapped = [first] + [across(made[1])] * (CHUNKS - 1)
    (other,) = hold([across(theirs)], 30 * 10**9)

    weights = []
    for chunk in range(CHUNKS):
        order = after(row_order, theirs, *weights)
        weights.append(
            score_rows(order, prompt_lengths, query, kv_cache, swapped[chunk], chunk)
        )
    moved = [lax.ppermute(made, "head", [(0, 2), (1, 3)]) for made in weights]

    blocks = along_z(after(mine, weights[-1]), other)
    crossed = [across(block, 2 * z) for z, block in enumerate(blocks[1:], 1)]
    blocks = [blocks[0], *hold(crossed, 10 * 10**9)]
    payload, rows = None, None
    for chunk in range(CHUNKS):
        cost = 10 * 10**9 if chunk + 1 == CHUNKS else 3 * 10**9
        payload, rows = mix_rows(
            after(row_order, weights[-1]), moved[chunk], kv_cache, swapped, chunk, payload, rows,
            cost,
        )
    parts = between_chips(payload)
    blocks = along_y([after(blocks[0], payload), *blocks[1:]])
    blocks = [blocks[0]] + [across(block, 8 * y) for y, block in enumerate(blocks[1:], 1)]
    low, high = combine(parts, att_query, new_kv)
    states = join_states([after(blocks[0], low), *blocks[1:]])
    states = states.reshape(wide_count, 2, heads, depth, width)
    states = states.transpose(1, 2, 0, 3, 4).reshape(2, heads, wide_count * depth, width)
    lin_out, final_states = delta_rule(
        states, lin_query, lin_key, lin_value, lin_decay, lin_beta, lin_gate
    )
    low_here, high_here = hold([lax.ppermute(low, "head", [(2, 0), (3, 2)]), lax.ppermute(high, "head", [(2, 1)])], 10 * 10**9)
    result = jnp.where(
        head_index == 3, high, jnp.where(head_index == 1, high_here, low_here)
    )
    gate = jnp.transpose(att_gate, (1, 0, 2)).astype(jnp.float32)
    att_out = (result * jax.nn.sigmoid(gate)).astype(jnp.bfloat16)
    att_out = jnp.transpose(att_out, (1, 0, 2))
    return (att_out, lin_out, final_states)


def solution(mesh):
    placed = (
        P(None, "wide", "head"),
        P(None, "head", "wide", None),
        P(),
        P(),
        P("wide", None, None, None),
        P("wide", None, None),
        P("wide", None, "head"),
        P("wide", None, "head", None),
        P("wide", None, "head", None),
        P("wide", None, "head", None),
        P("wide", None, "head"),
        P("wide", None, "head"),
        P("wide", None, "head", None),
    )
    return jax.shard_map(
        on_device,
        mesh=mesh,
        in_specs=placed,
        out_specs=(
            P("wide", None, "head"),
            P("wide", None, "head", None),
            P("wide", "head", None, None),
        ),
        check_vma=False,
    )
```

```python
import functools

import jax
import jax.numpy as jnp
from jax import lax
from jax.experimental import pallas as pl
from jax.experimental.pallas import tpu as pltpu
from jax.sharding import PartitionSpec as P

HQ = 16
KVH = 2
HD = 256
STEPS = 3
GROUP = HQ // KVH
QROWS = STEPS * GROUP
LANES = 128
NEGATIVE = -1e30

SLOTS = 32
SIZES = (10, 14, 8)
FIRSTS = (0, 10, 24)
CHUNKS = 3
GROUPS = ((10,), (6, 8), (8,))
NT = (((1,), (1,)), ((), ()))
LIMIT = 16 * 2**20
VMEM = pl.BlockSpec(memory_space=pltpu.VMEM)
SMEM = pl.BlockSpec(memory_space=pltpu.SMEM)
ANY = pl.BlockSpec(memory_space=pltpu.HBM)
PARAMS = pltpu.CompilerParams(vmem_limit_bytes=LIMIT)
FREE = pl.CostEstimate(flops=0, bytes_accessed=0, transcendentals=0)

def near(array):
    return pltpu.with_memory_space_constraint(array, pltpu.VMEM)


def far(array):
    return pltpu.with_memory_space_constraint(array, pltpu.HBM)


def prefill_row(order, slot, other=0):
    core = (lax.axis_index("wide") & 1) ^ other
    return order[4 * (slot // 2) + 2 * core + slot % 2]


def gather_kernel(order, cache, out, held, arrived, left, *, first):
    count = out.shape[0]
    reads = [
        pltpu.make_async_copy(cache.at[prefill_row(order, first + n, 1)], held.at[n], arrived.at[n])
        for n in range(count)
    ]
    writes = [pltpu.make_async_copy(held.at[n], out.at[n], left.at[n]) for n in range(count)]
    for read in reads:
        read.start()
    for read, write in zip(reads, writes):
        read.wait()
        write.start()
    for write in writes:
        write.wait()


def gather_rows(order, cache, first, count):
    copies = pltpu.SemaphoreType.DMA((count,))
    return pl.pallas_call(
        functools.partial(gather_kernel, first=first),
        name="gather_rows",
        out_shape=pltpu.HBM((count, *cache.shape[1:]), cache.dtype),
        in_specs=[SMEM, ANY],
        out_specs=ANY,
        scratch_shapes=[held_rows(cache, count), copies, copies],
        compiler_params=PARAMS,
        cost_estimate=FREE,
    )(far(order), far(cache))


def hold_kernel(*refs):
    pass


def hold(arrays, cost):
    count = len(arrays)
    return pl.pallas_call(
        hold_kernel,
        name="hold",
        out_shape=[pltpu.VMEM(array.shape, array.dtype) for array in arrays],
        in_specs=[VMEM] * count,
        out_specs=[VMEM] * count,
        input_output_aliases={n: n for n in range(count)},
        compiler_params=PARAMS,
        cost_estimate=pl.CostEstimate(flops=cost, bytes_accessed=0, transcendentals=0),
    )(*[near(array) for array in arrays])


def fetches(order, cache, swapped, own, other, arrived, chunk):
    groups, first = {}, 0
    base = FIRSTS[chunk] - FIRSTS[1]
    for at, size in enumerate(GROUPS[chunk]):
        copies = [
            pltpu.make_async_copy(
                cache.at[prefill_row(order, FIRSTS[chunk] + n)], own.at[n], arrived.at[n]
            )
            for n in range(first, first + size)
        ]
        if chunk:
            copies.insert(
                0,
                pltpu.make_async_copy(
                    swapped.at[pl.ds(base + first, size)],
                    other.at[pl.ds(first, size)],
                    arrived.at[SIZES[chunk] + at],
                ),
            )
        groups[first] = copies
        first += size
    return groups


def start(groups):
    for copies in groups.values():
        for copy in copies:
            copy.start()


def wait(groups, first):
    for copy in groups.get(first, ()):
        copy.wait()


def held_rows(cache, size):
    return pltpu.VMEM((size, *cache.shape[1:]), cache.dtype)


def arrivals(chunk):
    return pltpu.SemaphoreType.DMA((SIZES[chunk] + len(GROUPS[chunk]),))


def score_kernel(order, lengths, query, cache, swapped, out, own, other, arrived, *, chunk):
    if not chunk:
        other = swapped
    size = SIZES[chunk]
    span = own.shape[1]
    width = 2 * span

    @pl.when(lax.axis_index("head") < 2)
    def _():
        groups = fetches(order, cache, swapped, own, other, arrived, chunk)
        start(groups)
        lane = lax.broadcasted_iota(jnp.int32, (QROWS, LANES), 1)
        column = lax.broadcasted_iota(jnp.int32, (QROWS, span), 1)
        wide = lax.axis_index("wide")
        position = jnp.concatenate([column + wide * span, column + (wide ^ 1) * span], axis=1)
        extra = jnp.zeros((QROWS, LANES), jnp.float32)
        for n in range(size):
            wait(groups, n)
            slot = FIRSTS[chunk] + n
            q = query[slot]
            scores = jnp.concatenate(
                [
                    lax.dot_general(q, own[n], NT, preferred_element_type=jnp.float32),
                    lax.dot_general(q, other[n], NT, preferred_element_type=jnp.float32),
                ],
                axis=1,
            ) * (HD ** (-0.5))
            valid = position < lengths[prefill_row(order, slot)]
            scores = jnp.where(valid, scores, NEGATIVE)
            top = jnp.max(scores, axis=1, keepdims=True)
            top = top.astype(jnp.bfloat16).astype(jnp.float32)
            weights = jnp.where(valid, jnp.exp(scores - top), 0.0)
            total = jnp.sum(weights, axis=1, keepdims=True)
            coarse = total.astype(jnp.bfloat16).astype(jnp.float32)
            out[:, n * width : (n + 1) * width] = weights.astype(out.dtype)
            extra = jnp.where(lane == n, top, extra)
            extra = jnp.where(lane == n + size, coarse, extra)
            extra = jnp.where(lane == n + 2 * size, total - coarse, extra)
        out[:, size * width :] = extra.astype(out.dtype)


def score_rows(order, lengths, query, cache, swapped, chunk):
    size = SIZES[chunk]
    rows = held_rows(cache, size)
    return pl.pallas_call(
        functools.partial(score_kernel, chunk=chunk),
        name="score_rows",
        out_shape=pltpu.VMEM((QROWS, size * 2 * cache.shape[1] + LANES), jnp.bfloat16),
        in_specs=[SMEM, SMEM, VMEM, ANY, ANY if chunk else VMEM],
        out_specs=VMEM,
        scratch_shapes=[rows, rows, arrivals(chunk)],
        compiler_params=PARAMS,
        cost_estimate=FREE,
    )(far(order), far(lengths), near(query), far(cache), (far if chunk else near)(swapped))


LINES = 2 * QROWS
SLAB = 2 * LINES + 16
EXTRAS = 8


def mix_kernel(order, weights, cache, *refs, chunk):
    given, more = chunk > 0, chunk + 1 < CHUNKS
    refs = list(refs)
    own = refs.pop(0) if given else None
    other = refs.pop(0)
    swapped = refs.pop(0) if more else None
    if given:
        refs.pop(0)
    out = refs.pop(0)
    following = [refs.pop(0) for _ in range(2)] if more else []
    if not given:
        own, arrived = refs.pop(0), refs.pop(0)
    if more:
        arrived_next = refs.pop(0)
    made, left = refs
    size = SIZES[chunk]
    span = own.shape[1]
    width = 2 * span

    @pl.when(lax.axis_index("head") >= 2)
    def _():
        if not given:
            groups = fetches(order, cache, None, own, other, arrived, chunk)
            start(groups)
        if more:
            groups_next = fetches(order, cache, swapped, *following, arrived_next, chunk + 1)
            start(groups_next)
        extra = weights[:, size * width :].astype(jnp.float32)
        extra = jnp.concatenate([extra, jnp.zeros((LANES - QROWS, LANES), jnp.float32)], axis=0)
        extra = jnp.transpose(extra)
        blank = jnp.zeros((16 - 6, LANES), jnp.float32)
        for pair in range(size // 2):
            if not given:
                wait(groups, 2 * pair)
            rows, lines = [], []
            for n in (2 * pair, 2 * pair + 1):
                at = n * width
                rows.append(
                    jnp.dot(
                        weights[:, at : at + span], own[n], preferred_element_type=jnp.float32
                    )
                    + jnp.dot(
                        weights[:, at + span : at + width],
                        other[n],
                        preferred_element_type=jnp.float32,
                    )
                )
                lines += [extra[n + k * size : n + k * size + 1] for k in range(3)]
            slab = [row[:, :LANES] for row in rows] + [row[:, LANES:] for row in rows]
            made[pair] = jnp.concatenate([*slab, *lines, blank], axis=0).astype(made.dtype)
        copy = pltpu.make_async_copy(
            made, out.at[pl.ds(FIRSTS[chunk] // 2, size // 2)], left.at[0]
        )
        copy.start()
        copy.wait()
        if more:
            for first in groups_next:
                wait(groups_next, first)


def mix_rows(order, weights, cache, swapped, chunk, before, rows, cost):
    given, more = chunk > 0, chunk + 1 < CHUNKS
    size = SIZES[chunk]
    payload = pltpu.HBM((SLOTS // 2, SLAB, LANES), jnp.bfloat16)
    in_specs = [SMEM, VMEM, ANY]
    operands = [far(order), near(weights), far(cache)]
    for array in rows if given else [swapped[chunk]]:
        in_specs.append(VMEM)
        operands.append(near(array))
    if more:
        in_specs.append(ANY)
        operands.append(far(swapped[chunk + 1]))
    aliases = {}
    if given:
        in_specs.append(ANY)
        aliases = {len(operands): 0}
        operands.append(far(before))
    following = [held_rows(cache, SIZES[chunk + 1])] * 2 if more else []
    made = pl.pallas_call(
        functools.partial(mix_kernel, chunk=chunk),
        name="mix_rows",
        out_shape=[payload, *following],
        in_specs=in_specs,
        out_specs=[ANY] + [VMEM] * len(following),
        input_output_aliases=aliases,
        scratch_shapes=([] if given else [held_rows(cache, size), arrivals(chunk)])
        + ([arrivals(chunk + 1)] if more else [])
        + [pltpu.VMEM((size // 2, SLAB, LANES), jnp.bfloat16), pltpu.SemaphoreType.DMA((1,))],
        compiler_params=PARAMS,
        cost_estimate=pl.CostEstimate(flops=cost, bytes_accessed=0, transcendentals=0),
    )(*operands)
    return made[0], made[1:]


def combine_kernel(parts, query, fresh, low, high):
    @pl.when(lax.axis_index("head") >= 2)
    def _():
        chips = parts.shape[0]
        second = lax.axis_index("head") & 1
        half = KVH * HD
        extras = jnp.stack(
            [parts[chip, 2 * LINES :].astype(jnp.float32)[:EXTRAS] for chip in range(chips)]
        )
        tops = [extras[:, 3 * row] for row in range(2)]
        totals = [extras[:, 3 * row + 1] + extras[:, 3 * row + 2] for row in range(2)]
        step = lax.broadcasted_iota(jnp.int32, (QROWS, STEPS), 0) // GROUP
        time = lax.broadcasted_iota(jnp.int32, (QROWS, STEPS), 1)
        keep = time <= step
        scores, values = [], []
        for row in range(2):
            news = fresh[row].astype(jnp.float32)
            keys = jnp.where(second == 1, news[:, HD:half], news[:, :HD])
            values.append(jnp.where(second == 1, news[:, half + HD :], news[:, half : half + HD]))
            q = jnp.where(second == 1, query[row, :, GROUP:], query[row, :, :GROUP])
            q = q.reshape(QROWS, HD).astype(jnp.float32)
            columns = [
                jnp.sum(q * keys[t : t + 1], axis=1, keepdims=True) for t in range(STEPS)
            ]
            score = jnp.concatenate(columns, axis=1) * (HD ** (-0.5))
            scores.append(jnp.where(keep, score, NEGATIVE))
        lines, marks = [], []
        for row in range(2):
            top = jnp.max(tops[row], axis=0, keepdims=True)
            factors = jnp.exp(tops[row] - top)
            lines += [top, jnp.sum(factors * totals[row], axis=0, keepdims=True)]
            marks.append(factors)
        blank = jnp.zeros((LANES - 4 - 2 * chips, LANES), jnp.float32)
        columns = jnp.transpose(jnp.concatenate([*marks, *lines, blank], axis=0))[:QROWS]
        halves = []
        for row in range(2):
            at = 2 * chips + 2 * row
            cached = columns[:, at : at + 1]
            top = jnp.maximum(cached, jnp.max(scores[row], axis=1, keepdims=True))
            scale = jnp.exp(cached - top)
            probs = jnp.where(keep, jnp.exp(scores[row] - top), 0.0)
            total = columns[:, at + 1 : at + 2] * scale + jnp.sum(probs, axis=1, keepdims=True)
            probs = probs.astype(jnp.bfloat16).astype(jnp.float32)
            mixed = sum(probs[:, t : t + 1] * values[row][t : t + 1] for t in range(STEPS))
            first = row * QROWS
            sides = []
            for k in range(2):
                acc = jnp.zeros((QROWS, LANES), jnp.float32)
                for chip in range(chips):
                    span = slice(k * LINES + first, k * LINES + first + QROWS)
                    part = parts[chip, span].astype(jnp.float32)
                    at = row * chips + chip
                    acc = acc + columns[:, at : at + 1] * part
                sides.append(acc * scale + mixed[:, k * LANES : (k + 1) * LANES])
            halves.append(jnp.concatenate(sides, axis=1) / total)
        heads = GROUP // 2
        for row in range(2):
            for s in range(STEPS):
                for a in range(heads):
                    at = s * GROUP + a
                    span = slice(a * HD, (a + 1) * HD)
                    low[s, row : row + 1, span] = halves[row][at : at + 1]
                    high[s, row : row + 1, span] = halves[row][at + heads : at + heads + 1]


def combine(parts, query, fresh):
    heads = GROUP // 2
    shape = pltpu.VMEM((STEPS, 2, heads * HD), jnp.float32)
    return pl.pallas_call(
        combine_kernel,
        name="combine_parts",
        out_shape=(shape, shape),
        in_specs=[VMEM, VMEM, VMEM],
        out_specs=(VMEM, VMEM),
        compiler_params=PARAMS,
        cost_estimate=FREE,
    )(near(parts), near(query), near(fresh))


NEAR = 4


def block_kernel(*refs, moves):
    for target, at, source, place in moves:
        refs[target][at] = refs[source][place].astype(refs[target].dtype)


def move_blocks(name, arrays, shapes, moves):
    count = len(arrays)
    return pl.pallas_call(
        functools.partial(
            block_kernel, moves=[(count + t, at, source, place) for t, at, source, place in moves]
        ),
        name=name,
        out_shape=[pltpu.VMEM(shape, jnp.bfloat16) for shape in shapes],
        in_specs=[VMEM] * count,
        out_specs=[VMEM] * len(shapes),
        compiler_params=PARAMS,
        cost_estimate=FREE,
    )(*[near(array) for array in arrays])


def split_kernel(order, states, mine, theirs):
    wide = lax.axis_index("wide")
    for z in range(NEAR):
        for y in range(NEAR):
            chip = (wide >> 1) ^ (4 * y + z)
            for row in range(2):
                at = 4 * chip + 2 * (wide & 1) + row
                mine[z, y, row] = states[order[at]].astype(mine.dtype)
                theirs[z, y, row] = states[order[at ^ 2]].astype(theirs.dtype)


def split_states(order, states):
    shape = pltpu.VMEM((NEAR, NEAR, 2, *states.shape[1:]), jnp.bfloat16)
    return pl.pallas_call(
        split_kernel,
        name="split_states",
        out_shape=(shape, shape),
        in_specs=[SMEM, VMEM],
        out_specs=(VMEM, VMEM),
        compiler_params=PARAMS,
        cost_estimate=FREE,
    )(far(order), near(states))


def along_z(mine, other):
    shape = (2, *mine.shape[1:])
    moves = [(z, core, core, z) for z in range(NEAR) for core in range(2)]
    return move_blocks("pack_z", [mine, other], [shape] * NEAR, moves)


def along_y(blocks):
    shape = (NEAR, 2, *blocks[0].shape[2:])
    moves = [
        (y, (z, core), z, (core, y)) for y in range(NEAR) for z in range(NEAR) for core in range(2)
    ]
    return move_blocks("pack_y", blocks, [shape] * NEAR, moves)


def join_kernel(*refs):
    blocks, out = refs[:NEAR], refs[NEAR]
    wide = lax.axis_index("wide")
    for y in range(NEAR):
        for z in range(NEAR):
            for core in range(2):
                out[wide ^ (8 * y + 2 * z + core)] = blocks[y][z, core]


def join_states(blocks):
    shape = (2 * NEAR * NEAR, *blocks[0].shape[2:])
    return pl.pallas_call(
        join_kernel,
        name="join_states",
        out_shape=pltpu.VMEM(shape, jnp.bfloat16),
        in_specs=[VMEM] * NEAR,
        out_specs=VMEM,
        compiler_params=PARAMS,
        cost_estimate=FREE,
    )(*[near(block) for block in blocks])


def delta_kernel(decay, beta, states, query, key, value, gate, out, final, rows):
    batch, steps, heads_k, width = key.shape
    heads_v = value.shape[2]
    ratio = heads_v // heads_k
    keys_at = batch * steps * heads_k

    def column(row, step, head):
        return (row * steps + step) * heads_k + head

    rows[...] = jnp.zeros_like(rows)
    for row in range(batch):
        for step in range(steps):
            at = column(row, step, 0)
            q = query[row, step].astype(jnp.float32)
            k = key[row, step].astype(jnp.float32)
            q = q * lax.rsqrt(jnp.sum(q * q, -1, keepdims=True) + 1e-06) * width ** (-0.5)
            k = k * lax.rsqrt(jnp.sum(k * k, -1, keepdims=True) + 1e-06)
            rows[at : at + heads_k] = q
            rows[keys_at + at : keys_at + at + heads_k] = k
    columns = jnp.transpose(rows[...])
    shape = (width, value.shape[3])
    for row in range(batch):
        made = [[] for _ in range(steps)]
        values = [value[row, step].astype(jnp.float32) for step in range(steps)]
        for head in range(heads_k):
            both = range(head * ratio, (head + 1) * ratio)
            held = [states[row, one].astype(jnp.float32) for one in both]
            for step in range(steps):
                at = column(row, step, head)
                q = jnp.broadcast_to(columns[:, at : at + 1], shape)
                k = jnp.broadcast_to(columns[:, keys_at + at : keys_at + at + 1], shape)
                for n, one in enumerate(both):
                    rate = decay[row, step, one]
                    recalled = jnp.sum(k * held[n], axis=0, keepdims=True)
                    change = beta[row, step, one] * (
                        values[step][one : one + 1] - rate * recalled
                    )
                    held[n] = rate * held[n] + k * change
                    made[step].append(jnp.sum(q * held[n], axis=0, keepdims=True))
            for n, one in enumerate(both):
                final[row, one] = held[n]
        for step in range(steps):
            read = jnp.concatenate(made[step], axis=0)
            read = read * lax.rsqrt(jnp.mean(read * read, -1, keepdims=True) + 1e-06)
            level = gate[row, step].astype(jnp.float32)
            out[row, step] = (read * (level * jax.nn.sigmoid(level))).astype(out.dtype)


def delta_rule(states, query, key, value, decay, beta, gate):
    width = key.shape[-1]
    return pl.pallas_call(
        delta_kernel,
        name="delta_rule",
        out_shape=(
            jax.ShapeDtypeStruct(value.shape, jnp.bfloat16),
            jax.ShapeDtypeStruct(states.shape, jnp.float32),
        ),
        in_specs=[SMEM, SMEM] + [VMEM] * 5,
        out_specs=(VMEM, VMEM),
        scratch_shapes=[pltpu.VMEM((width, width), jnp.float32)],
        compiler_params=PARAMS,
        cost_estimate=FREE,
    )(decay, beta, states, query, key, value, gate)


def on_device(
    kv_cache,
    lin_states,
    row_order,
    prompt_lengths,
    att_query,
    new_kv,
    att_gate,
    lin_query,
    lin_key,
    lin_value,
    lin_decay,
    lin_beta,
    lin_gate,
):
    wide_count = lax.axis_size("wide")
    chips = wide_count // 2
    head_index = lax.axis_index("head")
    def across(array, distance=1):
        pairs = [(i, i ^ distance) for i in range(wide_count)]
        return lax.ppermute(array, "wide", pairs)

    def after(array, *others):
        return lax.optimization_barrier((array, *others))[0]

    same_core = [[2 * k + c for k in range(chips)] for c in range(2)]

    def between_chips(array):
        return lax.all_to_all(array, "wide", 0, 0, tiled=True, axis_index_groups=same_core)

    sides = [
        jnp.broadcast_to(side.reshape(1, 2, QROWS, HD), (chips, 2, QROWS, HD))
        for side in (att_query[:, :, :GROUP], att_query[:, :, GROUP:])
    ]
    copies = jnp.where(head_index % KVH == 1, sides[1], sides[0])
    (query,) = hold([between_chips(copies.reshape(2 * chips, QROWS, HD))], 30 * 10**9)

    first = gather_rows(row_order, kv_cache, 0, FIRSTS[1])
    made = [first, gather_rows(after(row_order, first), kv_cache, FIRSTS[1], SLOTS - FIRSTS[1])]
    rows_all, heads, depth, width = lin_states.shape
    mine, theirs = split_states(
        after(row_order, *made), lin_states.reshape(rows_all, heads * depth, width)
    )
    query, first = hold([query, across(made[0])], 30 * 10**9)
    swapped = [first] + [across(made[1])] * (CHUNKS - 1)
    (other,) = hold([across(theirs)], 30 * 10**9)

    weights = []
    for chunk in range(CHUNKS):
        order = after(row_order, theirs, *weights)
        weights.append(
            score_rows(order, prompt_lengths, query, kv_cache, swapped[chunk], chunk)
        )
    moved = [lax.ppermute(made, "head", [(0, 2), (1, 3)]) for made in weights]

    blocks = along_z(after(mine, weights[-1]), other)
    crossed = [across(block, 2 * z) for z, block in enumerate(blocks[1:], 1)]
    blocks = [blocks[0], *hold(crossed, 10 * 10**9)]
    payload, rows = None, None
    for chunk in range(CHUNKS):
        cost = 10 * 10**9 if chunk + 1 == CHUNKS else 3 * 10**9
        payload, rows = mix_rows(
            after(row_order, weights[-1]), moved[chunk], kv_cache, swapped, chunk, payload, rows,
            cost,
        )
    parts = between_chips(payload)
    blocks = along_y([after(blocks[0], payload), *blocks[1:]])
    blocks = [blocks[0]] + [across(block, 8 * y) for y, block in enumerate(blocks[1:], 1)]
    low, high = combine(parts, att_query, new_kv)
    states = join_states([after(blocks[0], low), *blocks[1:]])
    states = states.reshape(wide_count, 2, heads, depth, width)
    states = states.transpose(1, 2, 0, 3, 4).reshape(2, heads, wide_count * depth, width)
    lin_out, final_states = delta_rule(
        states, lin_query, lin_key, lin_value, lin_decay, lin_beta, lin_gate
    )
    low_here, high_here = hold([lax.ppermute(low, "head", [(2, 0), (3, 2)]), lax.ppermute(high, "head", [(2, 1)])], 10 * 10**9)
    result = jnp.where(
        head_index == 3, high, jnp.where(head_index == 1, high_here, low_here)
    )
    gate = jnp.transpose(att_gate, (1, 0, 2)).astype(jnp.float32)
    att_out = (result * jax.nn.sigmoid(gate)).astype(jnp.bfloat16)
    att_out = jnp.transpose(att_out, (1, 0, 2))
    return (att_out, lin_out, final_states)


def solution(mesh):
    placed = (
        P(None, "wide", "head"),
        P(None, "head", "wide", None),
        P(),
        P(),
        P("wide", None, None, None),
        P("wide", None, None),
        P("wide", None, "head"),
        P("wide", None, "head", None),
        P("wide", None, "head", None),
        P("wide", None, "head", None),
        P("wide", None, "head"),
        P("wide", None, "head"),
        P("wide", None, "head", None),
    )
    return jax.shard_map(
        on_device,
        mesh=mesh,
        in_specs=placed,
        out_specs=(
            P("wide", None, "head"),
            P("wide", None, "head", None),
            P("wide", "head", None, None),
        ),
        check_vma=False,
    )
```
